512 devices in a mesh: win: 8 (over x, y_lo), tile: 64 (over y_hi, z, core).
Axes of the slice: x: 4, y: 8 (y_hi: 4, y_lo: 2; y = y_hi * 2 + y_lo), z: 8, core: 2. Of those that a mesh axis runs over, the one named last changes fastest.
Arguments:
- increments: float32 [8, 16, 8192, 128], P('win', None, 'tile'), may hold values from -6 to 6
- multipliers: float32 [8, 16, 8192, 128], P('win', None, 'tile'), may hold values from -6 to 6
- departure_weight: float32 [8192, 128], P('tile'), may hold values from 0.2 to 0.8
- upstream: int32 [8192, 128], P('tile'), may hold values from -2 to 2
- level_offset: int32 [8192, 128], P('tile'), may hold values from -1 to 1
- diffusivity: float32 [8192, 128], P('tile'), may hold values from 0.02 to 0.24
- std_dev: float32 [8192, 128], P('tile'), may hold values from 0.5 to 2
- vertical_inverse: float32 [16, 16], replicated, may hold values from -0.1 to 1.2, as said below
Outputs:
- primal_out: float32 [8, 16, 8192, 128], P('win', None, 'tile')
- dual_out: float32 [8, 16, 8192, 128], P('win', None, 'tile')
The draws below stay inside these ranges and needn't reach their ends.
Inputs may be any that keep to these rules, and one draw needn't show every extreme that they name: `vertical_inverse`: A full-rank matrix with a diagonal near one and small off-diagonal entries of both signs.
All inputs are finite; a program needn't handle non-finite values.
Results may differ from the reference program's by a relative error of at most 0.0001.
Values sent between devices are 32-bit elements; how exact they have to be, the bound alone decides.
No kernel may reach another device: no remote copies, remote signals or barrier semaphores. Data moves between devices by JAX's collectives and lax.ppermute only.
A program may use at most 64 MiB of HBM per device.

```python
import math
import jax
import jax.numpy as jnp
from jax import lax

L = 16
NY = 128
SWEEPS = 4
SUBWIN = 8
NX = 8192


def draw_vertical_inverse(key, part):
    key = jax.random.fold_in(key, 11)
    diag_key, couple_key = jax.random.split(key)
    diagonal = jax.random.uniform(diag_key, (L,), jnp.float32, 0.8, 1.2)
    coupling = jax.random.uniform(couple_key, (L, L), jnp.float32, -0.08, 0.08)
    identity = jnp.eye(L, dtype=jnp.float32)
    return identity * diagonal[:, None] + (1.0 - identity) * coupling


def place_ends(entries, own_key, least, top_value):
    longest = entries.shape.index(max(entries.shape))
    spots = []
    for shift in (0, 1):
        where = [jax.random.randint(jax.random.fold_in(own_key, axis), (), 0, length) for axis, length in enumerate(entries.shape)]
        where[longest] = (where[longest] + shift) % entries.shape[longest]
        spots.append(tuple(where))
    return entries.at[spots[0]].set(least).at[spots[1]].set(top_value)


def block_levels(own_key, dims, cuts, least, largest):
    gain, own = 1.0, jax.random.fold_in(own_key, 6)
    for position, parts in cuts:
        heights = jnp.exp(jax.random.uniform(jax.random.fold_in(own, position), (parts,), jnp.float32, least / len(cuts), largest / len(cuts)))
        gain = gain * jnp.repeat(heights, dims[position] // parts).reshape([-1 if axis == position else 1 for axis in range(len(dims))])
    return gain


def noise(rng, dims, scale, reach, cuts=(), kind=jnp.bfloat16):
    entries = scale * jax.random.normal(rng, dims, jnp.float32)
    if cuts:
        entries = entries * block_levels(rng, dims, cuts, -0.22, 0.18)
    return jnp.clip(entries, -reach, reach).astype(kind)


def setup_inputs(seed: int = 0) -> dict:
    keys = jax.random.split(jax.random.key(seed), 9)
    return {
        "increments": noise(keys[0], (SUBWIN, L, NX, NY), 1.0, 6.0, ((0, 8), (2, 64)), jnp.float32),
        "multipliers": noise(keys[1], (SUBWIN, L, NX, NY), 1.0, 6.0, ((0, 8), (2, 64)), jnp.float32),
        "departure_weight": jnp.clip(0.2 + 0.6 * jax.random.uniform(keys[2], (NX, NY), jnp.float32) ** block_levels(keys[2], (NX, NY), ((0, 64),), -0.2, 0.2), 0.2, 0.8),
        "upstream": place_ends(jax.random.randint(keys[3], (NX, NY), -2, 3), jax.random.fold_in(keys[3], 1), -2, 2).astype(jnp.int32),
        "level_offset": place_ends(jax.random.randint(keys[4], (NX, NY), -1, 2), jax.random.fold_in(keys[4], 1), -1, 1).astype(jnp.int32),
        "diffusivity": jnp.clip(jnp.exp(math.log(0.24) - 2.4849066 * jax.random.uniform(keys[5], (NX, NY), jnp.float32) ** block_levels(keys[5], (NX, NY), ((0, 64),), -0.2, 0.2)), 0.02, 0.24),
        "std_dev": jnp.clip(jnp.exp(math.log(2.0) - 1.3862944 * jax.random.uniform(keys[6], (NX, NY), jnp.float32) ** block_levels(keys[6], (NX, NY), ((0, 64),), -0.2, 0.2)), 0.5, 2.0),
        "vertical_inverse": draw_vertical_inverse(jax.random.fold_in(keys[8], 71), 0),
    }


def level_shift(values, level_step):
    if level_step == 0:
        return values
    zero_row = jnp.zeros_like(values[:1])
    if level_step > 0:
        return jnp.concatenate([values[level_step:], zero_row], 0)
    return jnp.concatenate([zero_row, values[:level_step]], 0)


def advect(values, departure_weight, upstream, level_offset):
    departed = jnp.zeros_like(values)
    for shift_x in range(-2, 3):
        rolled = jnp.roll(values, -shift_x, axis=1)
        for shift_z in (-1, 0, 1):
            selector = ((upstream == shift_x) & (level_offset == shift_z)).astype(values.dtype)
            departed = departed + selector * level_shift(rolled, shift_z)
    return (1.0 - departure_weight) * values + departure_weight * departed


def advect_adjoint(values, departure_weight, upstream, level_offset):
    returned = jnp.zeros_like(values)
    for shift_x in range(-2, 3):
        for shift_z in (-1, 0, 1):
            selector = ((upstream == shift_x) & (level_offset == shift_z)).astype(values.dtype)
            source = (selector * departure_weight) * level_shift(values, -shift_z)
            returned = returned + jnp.roll(source, shift_x, axis=1)
    return (1.0 - departure_weight) * values + returned


def diffuse(values, diffusivity, vertical_inverse):
    zero_row = jnp.zeros_like(values[:, :, :1])
    northern = jnp.concatenate([values[:, :, 1:], zero_row], 2)
    southern = jnp.concatenate([zero_row, values[:, :, :-1]], 2)
    eastern = jnp.roll(values, -1, axis=1)
    western = jnp.roll(values, 1, axis=1)
    smooth = values + diffusivity * (eastern + western - 2.0 * values) + diffusivity * (northern + southern - 2.0 * values)
    level_count, column_count, row_count = smooth.shape
    blended = jnp.dot(vertical_inverse, smooth.reshape(level_count, column_count * row_count), precision=lax.Precision.HIGHEST, preferred_element_type=jnp.float32)
    return blended.reshape(level_count, column_count, row_count)


def reference(increments, multipliers, departure_weight, upstream, level_offset, diffusivity, std_dev, vertical_inverse):
    windows = increments.shape[0]
    primal_rows = []
    dual_rows = []
    for index in range(windows):
        smoothed = std_dev * multipliers[index]
        for sweep_index in range(SWEEPS):
            smoothed = diffuse(smoothed, diffusivity, vertical_inverse)
        primal_row = std_dev * smoothed + increments[index]
        if index > 0:
            primal_row = primal_row - advect(increments[index - 1], departure_weight, upstream, level_offset)
        dual_row = multipliers[index]
        if index < windows - 1:
            dual_row = dual_row - advect_adjoint(multipliers[index + 1], departure_weight, upstream, level_offset)
        primal_rows.append(primal_row)
        dual_rows.append(dual_row)
    return jnp.stack(primal_rows), jnp.stack(dual_rows)
```

```python
import functools

import jax
import jax.numpy as jnp
from jax import lax
from jax.experimental import pallas as pl
from jax.experimental.pallas import tpu as pltpu
from jax.sharding import PartitionSpec as P

SWEEPS = 4
REACH = 2
PAD = 8
EARLY = 1080
VMEM_LIMIT = 40 * 1024 * 1024
VMEM_WHOLE = 60 * 1024 * 1024


def moved(value, win_by, tile_by):
    wins, tiles = lax.axis_size("win"), lax.axis_size("tile")
    pairs = [
        (k * tiles + t, (k + win_by) * tiles + (t + tile_by) % tiles)
        for k in range(wins)
        for t in range(tiles)
        if 0 <= k + win_by < wins
    ]
    return lax.ppermute(value, ("win", "tile"), pairs)


def params():
    return pltpu.CompilerParams(vmem_limit_bytes=VMEM_LIMIT)


def cost(flops, touched):
    return pl.CostEstimate(flops=flops, bytes_accessed=touched, transcendentals=0)


class Rows:
    def __init__(self, levels):
        base = SWEEPS * levels
        self.std = slice(base, base + SWEEPS)
        self.kappa = slice(base + SWEEPS, base + 2 * SWEEPS)
        self.weight = slice(base + 2 * SWEEPS, base + 2 * SWEEPS + REACH)
        self.code = slice(base + 2 * SWEEPS + REACH, base + 2 * SWEEPS + 2 * REACH)
        self.fields = base + 4 * SWEEPS
        self.count = self.fields + REACH * levels

    def mul(self, l):
        return slice(SWEEPS * l, SWEEPS * (l + 1))

    def inc(self, l):
        return slice(self.fields + REACH * l, self.fields + REACH * (l + 1))


def pack_one(levels, refs, out, from_end):
    inc, mul, std, kappa, weight, up, lev = refs
    wide = slice(PAD - SWEEPS, PAD) if from_end else slice(0, SWEEPS)
    thin = slice(PAD - REACH, PAD) if from_end else slice(0, REACH)
    spot = Rows(levels)
    for l in range(levels):
        out[spot.mul(l)] = mul[0, l, wide]
        out[spot.inc(l)] = inc[0, l, thin]
    out[spot.std] = std[wide]
    out[spot.kappa] = kappa[wide]
    out[spot.weight] = weight[thin]
    out[spot.code] = up[thin].astype(jnp.float32) * 3.0 + lev[thin].astype(jnp.float32)
    gap = slice(spot.code.stop, spot.fields)
    out[gap] = jnp.zeros_like(out[gap])


def pack_both(levels, *refs):
    pack_one(levels, refs[0:7], refs[14], True)
    pack_one(levels, refs[7:14], refs[15], False)


def pack(inc, mul, std, kappa, weight, up, lev):
    _, levels, width, rows = mul.shape
    arrays = [inc, mul, std, kappa, weight, up, lev]
    specs = []
    for block in (width // PAD - 1, 0):
        for a in arrays:
            lead = a.shape[:-2]
            index = (0,) * len(lead) + (block, 0)
            specs.append(
                pl.BlockSpec((*lead, PAD, rows), functools.partial(lambda index, i: index, index))
            )
    height = Rows(levels).count
    return pl.pallas_call(
        functools.partial(pack_both, levels),
        grid=(1,),
        in_specs=specs,
        out_specs=[pl.BlockSpec((height, rows), lambda i: (0, 0))] * 2,
        out_shape=[jax.ShapeDtypeStruct((height, rows), jnp.float32)] * 2,
        compiler_params=pltpu.CompilerParams(vmem_limit_bytes=VMEM_WHOLE),
        cost_estimate=cost(1000, 1000),
    )(*(arrays * 2))


def forward_kernel(early, inc, mul, before, after, inc_out, mul_out):
    _, levels, width, rows = mul.shape
    spot = Rows(levels)
    base, half = levels * width - early, REACH * levels
    for l in range(levels):
        start = max(early - l * width, 0)
        if start < width:
            part = slice(l * width + start - early, (l + 1) * width - early)
            inc_out[part] = inc[0, l, start:]
            mul_out[part] = mul[0, l, start:]
    for l in range(levels):
        near = slice(base + REACH * l, base + REACH * (l + 1))
        far = slice(near.start + half, near.stop + half)
        first, last = before[spot.mul(l)], after[spot.mul(l)]
        mul_out[near] = first[SWEEPS - REACH :]
        mul_out[far] = last[:REACH]
        inc_out[near] = before[spot.inc(l)]
        inc_out[far] = after[spot.inc(l)]


def forward(early, inc, mul, before, after):
    _, levels, width, rows = mul.shape
    vmem = pl.BlockSpec(memory_space=pltpu.VMEM)
    height = levels * width - early + 2 * REACH * levels
    return pl.pallas_call(
        functools.partial(forward_kernel, early),
        in_specs=[vmem] * 4,
        out_specs=[vmem] * 2,
        out_shape=[jax.ShapeDtypeStruct((height, rows), jnp.float32)] * 2,
        compiler_params=params(),
        cost_estimate=cost(1000, 1000),
    )(inc, mul, before, after)


def covar_kernel(
    mul, inc, std, kappa, before, after, power, out, kappa_ext, field, smooth
):
    levels, width, rows = smooth.shape
    tall = width + 2 * PAD
    spot = Rows(levels)
    kappa_ext[...] = jnp.zeros_like(kappa_ext)
    field[...] = jnp.zeros_like(field)
    kappa_ext[PAD : PAD + width] = kappa[...]
    kappa_ext[PAD - SWEEPS : PAD] = before[spot.kappa]
    kappa_ext[PAD + width : PAD + width + SWEEPS] = after[spot.kappa]
    for l in range(levels):
        field[l, PAD - SWEEPS : PAD] = before[spot.std] * before[spot.mul(l)]
        field[l, PAD + width : PAD + width + SWEEPS] = after[spot.std] * after[spot.mul(l)]
    lane = lax.broadcasted_iota(jnp.int32, (tall, rows), 1)
    first, last = lane == 0, lane == rows - 1

    def one_level(l, carry):
        field[l, PAD : PAD + width] = std[...] * mul[0, l]
        value = field[l]
        for _ in range(SWEEPS):
            north = jnp.where(last, 0.0, pltpu.roll(value, rows - 1, 1))
            south = jnp.where(first, 0.0, pltpu.roll(value, 1, 1))
            around = pltpu.roll(value, 1, 0) + pltpu.roll(value, tall - 1, 0)
            value = value + kappa_ext[...] * ((around + (north + south)) - 4.0 * value)
        smooth[l] = value[PAD : PAD + width]
        return carry

    lax.fori_loop(0, levels, one_level, 0)
    step = 2 * PAD

    def one_block(b, carry):
        part = pl.ds(pl.multiple_of(b * step, step), step)
        fields = [smooth[m, part] for m in range(levels)]
        scale = std[part]
        for l in range(levels):
            total = power[l, 0] * fields[0]
            for m in range(1, levels):
                total = total + power[l, m] * fields[m]
            out[l, part] = scale * total + inc[0, l, part]
        return carry

    lax.fori_loop(0, width // step, one_block, 0)


def covar(mul, inc, std, kappa, before, after, power):
    _, levels, width, rows = mul.shape
    vmem = pl.BlockSpec(memory_space=pltpu.VMEM)
    return pl.pallas_call(
        covar_kernel,
        in_specs=[vmem] * 6 + [pl.BlockSpec(memory_space=pltpu.SMEM)],
        out_specs=vmem,
        out_shape=jax.ShapeDtypeStruct((levels, width, rows), jnp.float32),
        scratch_shapes=[
            pltpu.VMEM((width + 2 * PAD, rows), jnp.float32),
            pltpu.VMEM((levels, width + 2 * PAD, rows), jnp.float32),
            pltpu.VMEM((levels, width, rows), jnp.float32),
        ],
        compiler_params=params(),
        cost_estimate=cost(1000, 1000),
    )(mul, inc, std, kappa, before, after, power)


def fill_field(field, offset, width, first, rest):
    early = first.shape[0]
    levels = field.shape[0] - 2 * offset
    base, half = levels * width - early, REACH * levels
    for l in range(levels):
        begin, end = l * width, (l + 1) * width
        cut = min(max(early, begin), end)
        if cut > begin:
            field[l + offset, PAD : PAD + cut - begin] = first[begin:cut]
        if cut < end:
            part = slice(PAD + cut - begin, PAD + width)
            field[l + offset, part] = rest[cut - early : end - early]
        near = slice(base + REACH * l, base + REACH * (l + 1))
        field[l + offset, PAD - REACH : PAD] = rest[near]
        far = rest[near.start + half : near.stop + half]
        field[l + offset, PAD + width : PAD + width + REACH] = far


def primal_kernel(base, came_first, came, weight, up, lev, out, field, level_field):
    levels, width, rows = base.shape
    fill_field(field, 0, width, came_first, came)
    zero = jnp.zeros((width, rows), jnp.float32)
    level_field[0] = zero
    level_field[levels + 1] = zero

    def one_level(l, carry):
        step = up[...]
        total = field[l, PAD : PAD + width]
        for j in (-2, -1, 1, 2):
            total = jnp.where(step == j, field[l, PAD + j : PAD + j + width], total)
        level_field[l + 1] = total
        return carry

    lax.fori_loop(0, levels, one_level, 0)

    def combine(l, carry):
        pick = lev[...]
        departed = jnp.where(
            pick == 0,
            level_field[l + 1],
            jnp.where(pick == 1, level_field[l + 2], level_field[l]),
        )
        center = field[l, PAD : PAD + width]
        out[0, l] = base[l] - ((1.0 - weight[...]) * center + weight[...] * departed)
        return carry

    lax.fori_loop(0, levels, combine, 0)


def primal_final(base, came_first, came, weight, up, lev):
    levels, width, rows = base.shape
    vmem = pl.BlockSpec(memory_space=pltpu.VMEM)
    return pl.pallas_call(
        primal_kernel,
        in_specs=[vmem] * 6,
        out_specs=vmem,
        out_shape=jax.ShapeDtypeStruct((1, levels, width, rows), jnp.float32),
        scratch_shapes=[
            pltpu.VMEM((levels, width + 2 * PAD, rows), jnp.float32),
            pltpu.VMEM((levels + 2, width, rows), jnp.float32),
        ],
        compiler_params=params(),
        cost_estimate=cost(1000, 1000),
    )(base, came_first, came, weight, up, lev)


def dual_kernel(
    mul, came_first, came, before, after, weight, up, lev, out, field, weight_ext, up_ext, lev_ext
):
    _, levels, width, rows = mul.shape
    tall = width + 2 * PAD
    spot = Rows(levels)
    left, right = slice(PAD - REACH, PAD), slice(PAD + width, PAD + width + REACH)
    weight_ext[...] = jnp.zeros_like(weight_ext)
    up_ext[...] = jnp.zeros_like(up_ext)
    lev_ext[...] = jnp.zeros_like(lev_ext)
    weight_ext[PAD : PAD + width] = weight[...]
    up_ext[PAD : PAD + width] = up[...]
    lev_ext[PAD : PAD + width] = lev[...]
    zero = jnp.zeros((tall, rows), jnp.float32)
    field[0] = zero
    field[levels + 1] = zero
    for side, part in ((before, left), (after, right)):
        weight_ext[part] = side[spot.weight]
        code = side[spot.code]
        step = jnp.floor((code + 1.5) * (1.0 / 3.0))
        up_ext[part] = step.astype(jnp.int32)
        lev_ext[part] = (code - 3.0 * step).astype(jnp.int32)
    for l in range(levels):
        field[l + 1, :PAD] = zero[:PAD]
        field[l + 1, PAD + width :] = zero[:PAD]
    fill_field(field, 1, width, came_first, came)

    def one_level(l, carry):
        pick = lev_ext[...]
        lifted = jnp.where(
            pick == 0, field[l + 1], jnp.where(pick == 1, field[l], field[l + 2])
        )
        source = weight_ext[...] * lifted
        step = up_ext[...]
        total = jnp.where(step == 0, source, 0.0)
        for j in (-2, -1, 1, 2):
            total = total + pltpu.roll(jnp.where(step == j, source, 0.0), j % tall, 0)
        returned = total[PAD : PAD + width]
        center = field[l + 1, PAD : PAD + width]
        out[0, l] = mul[0, l] - ((1.0 - weight[...]) * center + returned)
        return carry

    lax.fori_loop(0, levels, one_level, 0)


def dual_final(mul, came_first, came, before, after, weight, up, lev):
    _, levels, width, rows = mul.shape
    vmem = pl.BlockSpec(memory_space=pltpu.VMEM)
    tall = width + 2 * PAD
    return pl.pallas_call(
        dual_kernel,
        in_specs=[vmem] * 8,
        out_specs=vmem,
        out_shape=jax.ShapeDtypeStruct((1, levels, width, rows), jnp.float32),
        scratch_shapes=[
            pltpu.VMEM((levels + 2, tall, rows), jnp.float32),
            pltpu.VMEM((tall, rows), jnp.float32),
            pltpu.VMEM((tall, rows), jnp.int32),
            pltpu.VMEM((tall, rows), jnp.int32),
        ],
        compiler_params=params(),
        cost_estimate=cost(1000, 1000),
    )(mul, came_first, came, before, after, weight, up, lev)


def per_device(
    increments,
    multipliers,
    departure_weight,
    upstream,
    level_offset,
    diffusivity,
    std_dev,
    vertical_inverse,
):
    columns = (departure_weight, upstream, level_offset)
    _, levels, width, rows = multipliers.shape
    early = EARLY * levels * width // 2048
    inc_first = moved(increments.reshape(-1, rows)[:early], 1, 0)
    mul_first = moved(multipliers.reshape(-1, rows)[:early], -1, 0)
    to_right, to_left = pack(increments, multipliers, std_dev, diffusivity, *columns)
    before = moved(to_right, 0, 1)
    after = moved(to_left, 0, -1)
    inc_out, mul_out = forward(early, increments, multipliers, before, after)
    inc_rest = moved(inc_out, 1, 0)
    mul_rest = moved(mul_out, -1, 0)

    exact = dict(precision=lax.Precision.HIGHEST, preferred_element_type=jnp.float32)
    power = jnp.dot(vertical_inverse, vertical_inverse, **exact)
    power = jnp.dot(power, power, **exact)
    base = covar(multipliers, increments, std_dev, diffusivity, before, after, power)
    primal = primal_final(base, inc_first, inc_rest, *columns)
    weight, primal = lax.optimization_barrier((departure_weight, primal))
    dual = dual_final(
        multipliers, mul_first, mul_rest, before, after, weight, upstream, level_offset
    )
    return (primal, dual)


def solution(mesh):
    in_specs = (
        P("win", None, "tile", None),
        P("win", None, "tile", None),
        P("tile", None),
        P("tile", None),
        P("tile", None),
        P("tile", None),
        P("tile", None),
        P(),
    )
    out_specs = (P("win", None, "tile", None), P("win", None, "tile", None))
    return jax.shard_map(
        per_device, mesh=mesh, in_specs=in_specs, out_specs=out_specs, check_vma=False
    )
```

```python
import functools

import jax
import jax.numpy as jnp
from jax import lax
from jax.experimental import pallas as pl
from jax.experimental.pallas import tpu as pltpu
from jax.sharding import PartitionSpec as P

SWEEPS = 4
REACH = 2
PAD = 8
EARLY = 1080
LEAD = 1280
VMEM_LIMIT = 40 * 1024 * 1024
VMEM_WHOLE = 60 * 1024 * 1024


def moved(value, win_by, tile_by):
    wins, tiles = lax.axis_size("win"), lax.axis_size("tile")
    pairs = [
        (k * tiles + t, (k + win_by) * tiles + (t + tile_by) % tiles)
        for k in range(wins)
        for t in range(tiles)
        if 0 <= k + win_by < wins
    ]
    return lax.ppermute(value, ("win", "tile"), pairs)


def params():
    return pltpu.CompilerParams(vmem_limit_bytes=VMEM_LIMIT)


def cost(flops, touched):
    return pl.CostEstimate(flops=flops, bytes_accessed=touched, transcendentals=0)


class Rows:
    def __init__(self, levels):
        base = SWEEPS * levels
        self.std = slice(base, base + SWEEPS)
        self.kappa = slice(base + SWEEPS, base + 2 * SWEEPS)
        self.weight = slice(base + 2 * SWEEPS, base + 2 * SWEEPS + REACH)
        self.code = slice(base + 2 * SWEEPS + REACH, base + 2 * SWEEPS + 2 * REACH)
        self.fields = base + 4 * SWEEPS
        self.count = self.fields + REACH * levels

    def mul(self, l):
        return slice(SWEEPS * l, SWEEPS * (l + 1))

    def inc(self, l):
        return slice(self.fields + REACH * l, self.fields + REACH * (l + 1))


def pack_one(levels, refs, out, from_end):
    inc, mul, std, kappa, weight, up, lev = refs
    wide = slice(PAD - SWEEPS, PAD) if from_end else slice(0, SWEEPS)
    thin = slice(PAD - REACH, PAD) if from_end else slice(0, REACH)
    spot = Rows(levels)
    for l in range(levels):
        out[spot.mul(l)] = mul[0, l, wide]
        out[spot.inc(l)] = inc[0, l, thin]
    out[spot.std] = std[wide]
    out[spot.kappa] = kappa[wide]
    out[spot.weight] = weight[thin]
    out[spot.code] = up[thin].astype(jnp.float32) * 3.0 + lev[thin].astype(jnp.float32)
    gap = slice(spot.code.stop, spot.fields)
    out[gap] = jnp.zeros_like(out[gap])


def pack_both(levels, *refs):
    pack_one(levels, refs[0:7], refs[14], True)
    pack_one(levels, refs[7:14], refs[15], False)


def pack(inc, mul, std, kappa, weight, up, lev):
    _, levels, width, rows = mul.shape
    arrays = [inc, mul, std, kappa, weight, up, lev]
    specs = []
    for block in (width // PAD - 1, 0):
        for a in arrays:
            lead = a.shape[:-2]
            index = (0,) * len(lead) + (block, 0)
            specs.append(
                pl.BlockSpec((*lead, PAD, rows), functools.partial(lambda index, i: index, index))
            )
    height = Rows(levels).count
    return pl.pallas_call(
        functools.partial(pack_both, levels),
        grid=(1,),
        in_specs=specs,
        out_specs=[pl.BlockSpec((height, rows), lambda i: (0, 0))] * 2,
        out_shape=[jax.ShapeDtypeStruct((height, rows), jnp.float32)] * 2,
        compiler_params=pltpu.CompilerParams(vmem_limit_bytes=VMEM_WHOLE),
        cost_estimate=cost(1000, 1000),
    )(*(arrays * 2))


def forward_kernel(inc_early, mul_early, inc, mul, before, after, inc_out, mul_out):
    _, levels, width, rows = mul.shape
    spot = Rows(levels)
    half = REACH * levels
    for early, source, target in ((inc_early, inc, inc_out), (mul_early, mul, mul_out)):
        base = levels * width - early
        for l in range(levels):
            start = max(early - l * width, 0)
            if start < width:
                part = slice(l * width + start - early, (l + 1) * width - early)
                target[part] = source[0, l, start:]
            near = slice(base + REACH * l, base + REACH * (l + 1))
            far = slice(near.start + half, near.stop + half)
            if source is inc:
                target[near] = before[spot.inc(l)]
                target[far] = after[spot.inc(l)]
            else:
                first, last = before[spot.mul(l)], after[spot.mul(l)]
                target[near] = first[SWEEPS - REACH :]
                target[far] = last[:REACH]


def forward(inc_early, mul_early, inc, mul, before, after):
    _, levels, width, rows = mul.shape
    vmem = pl.BlockSpec(memory_space=pltpu.VMEM)
    heights = [levels * width - early + 2 * REACH * levels for early in (inc_early, mul_early)]
    return pl.pallas_call(
        functools.partial(forward_kernel, inc_early, mul_early),
        in_specs=[vmem] * 4,
        out_specs=[vmem] * 2,
        out_shape=[jax.ShapeDtypeStruct((h, rows), jnp.float32) for h in heights],
        compiler_params=params(),
        cost_estimate=cost(1000, 1000),
    )(inc, mul, before, after)


def covar_kernel(
    mul, inc, std, kappa, before, after, power, out, kappa_ext, field, smooth
):
    levels, width, rows = smooth.shape
    tall = width + 2 * PAD
    spot = Rows(levels)
    kappa_ext[...] = jnp.zeros_like(kappa_ext)
    field[...] = jnp.zeros_like(field)
    kappa_ext[PAD : PAD + width] = kappa[...]
    kappa_ext[PAD - SWEEPS : PAD] = before[spot.kappa]
    kappa_ext[PAD + width : PAD + width + SWEEPS] = after[spot.kappa]
    for l in range(levels):
        field[l, PAD - SWEEPS : PAD] = before[spot.std] * before[spot.mul(l)]
        field[l, PAD + width : PAD + width + SWEEPS] = after[spot.std] * after[spot.mul(l)]
    lane = lax.broadcasted_iota(jnp.int32, (tall, rows), 1)
    first, last = lane == 0, lane == rows - 1

    def one_level(l, carry):
        field[l, PAD : PAD + width] = std[...] * mul[0, l]
        value = field[l]
        for _ in range(SWEEPS):
            north = jnp.where(last, 0.0, pltpu.roll(value, rows - 1, 1))
            south = jnp.where(first, 0.0, pltpu.roll(value, 1, 1))
            around = pltpu.roll(value, 1, 0) + pltpu.roll(value, tall - 1, 0)
            value = value + kappa_ext[...] * ((around + (north + south)) - 4.0 * value)
        smooth[l] = value[PAD : PAD + width]
        return carry

    lax.fori_loop(0, levels, one_level, 0)
    step = 2 * PAD

    def one_block(b, carry):
        part = pl.ds(pl.multiple_of(b * step, step), step)
        fields = [smooth[m, part] for m in range(levels)]
        scale = std[part]
        for l in range(levels):
            total = power[l, 0] * fields[0]
            for m in range(1, levels):
                total = total + power[l, m] * fields[m]
            out[l, part] = scale * total + inc[0, l, part]
        return carry

    lax.fori_loop(0, width // step, one_block, 0)


def covar(mul, inc, std, kappa, before, after, power):
    _, levels, width, rows = mul.shape
    vmem = pl.BlockSpec(memory_space=pltpu.VMEM)
    return pl.pallas_call(
        covar_kernel,
        in_specs=[vmem] * 6 + [pl.BlockSpec(memory_space=pltpu.SMEM)],
        out_specs=vmem,
        out_shape=jax.ShapeDtypeStruct((levels, width, rows), jnp.float32),
        scratch_shapes=[
            pltpu.VMEM((width + 2 * PAD, rows), jnp.float32),
            pltpu.VMEM((levels, width + 2 * PAD, rows), jnp.float32),
            pltpu.VMEM((levels, width, rows), jnp.float32),
        ],
        compiler_params=params(),
        cost_estimate=cost(1000, 1000),
    )(mul, inc, std, kappa, before, after, power)


def fill_field(field, offset, width, *pieces):
    levels = field.shape[0] - 2 * offset
    rest, half = pieces[-1], REACH * levels
    base = rest.shape[0] - 2 * half
    start = 0
    for piece in pieces:
        stop = start + (base if piece is rest else piece.shape[0])
        for l in range(levels):
            begin, end = max(l * width, start), min((l + 1) * width, stop)
            if begin < end:
                part = slice(PAD + begin - l * width, PAD + end - l * width)
                field[l + offset, part] = piece[begin - start : end - start]
        start = stop
    for l in range(levels):
        near = slice(base + REACH * l, base + REACH * (l + 1))
        field[l + offset, PAD - REACH : PAD] = rest[near]
        far = rest[near.start + half : near.stop + half]
        field[l + offset, PAD + width : PAD + width + REACH] = far


def primal_kernel(base, came_first, came, weight, up, lev, out, field, level_field):
    levels, width, rows = base.shape
    fill_field(field, 0, width, came_first, came)
    zero = jnp.zeros((width, rows), jnp.float32)
    level_field[0] = zero
    level_field[levels + 1] = zero

    def one_level(l, carry):
        step = up[...]
        total = field[l, PAD : PAD + width]
        for j in (-2, -1, 1, 2):
            total = jnp.where(step == j, field[l, PAD + j : PAD + j + width], total)
        level_field[l + 1] = total
        return carry

    lax.fori_loop(0, levels, one_level, 0)

    def combine(l, carry):
        pick = lev[...]
        departed = jnp.where(
            pick == 0,
            level_field[l + 1],
            jnp.where(pick == 1, level_field[l + 2], level_field[l]),
        )
        center = field[l, PAD : PAD + width]
        out[0, l] = base[l] - ((1.0 - weight[...]) * center + weight[...] * departed)
        return carry

    lax.fori_loop(0, levels, combine, 0)


def primal_final(base, came_first, came, weight, up, lev):
    levels, width, rows = base.shape
    vmem = pl.BlockSpec(memory_space=pltpu.VMEM)
    return pl.pallas_call(
        primal_kernel,
        in_specs=[vmem] * 6,
        out_specs=vmem,
        out_shape=jax.ShapeDtypeStruct((1, levels, width, rows), jnp.float32),
        scratch_shapes=[
            pltpu.VMEM((levels, width + 2 * PAD, rows), jnp.float32),
            pltpu.VMEM((levels + 2, width, rows), jnp.float32),
        ],
        compiler_params=params(),
        cost_estimate=cost(1000, 1000),
    )(base, came_first, came, weight, up, lev)


def dual_kernel(
    mul, came_first, came, before, after, weight, up, lev, out, field, weight_ext, up_ext, lev_ext
):
    _, levels, width, rows = mul.shape
    tall = width + 2 * PAD
    spot = Rows(levels)
    left, right = slice(PAD - REACH, PAD), slice(PAD + width, PAD + width + REACH)
    weight_ext[...] = jnp.zeros_like(weight_ext)
    up_ext[...] = jnp.zeros_like(up_ext)
    lev_ext[...] = jnp.zeros_like(lev_ext)
    weight_ext[PAD : PAD + width] = weight[...]
    up_ext[PAD : PAD + width] = up[...]
    lev_ext[PAD : PAD + width] = lev[...]
    zero = jnp.zeros((tall, rows), jnp.float32)
    field[0] = zero
    field[levels + 1] = zero
    for side, part in ((before, left), (after, right)):
        weight_ext[part] = side[spot.weight]
        code = side[spot.code]
        step = jnp.floor((code + 1.5) * (1.0 / 3.0))
        up_ext[part] = step.astype(jnp.int32)
        lev_ext[part] = (code - 3.0 * step).astype(jnp.int32)
    for l in range(levels):
        field[l + 1, :PAD] = zero[:PAD]
        field[l + 1, PAD + width :] = zero[:PAD]
    fill_field(field, 1, width, came_first, came)

    def one_level(l, carry):
        pick = lev_ext[...]
        lifted = jnp.where(
            pick == 0, field[l + 1], jnp.where(pick == 1, field[l], field[l + 2])
        )
        source = weight_ext[...] * lifted
        step = up_ext[...]
        total = jnp.where(step == 0, source, 0.0)
        for j in (-2, -1, 1, 2):
            total = total + pltpu.roll(jnp.where(step == j, source, 0.0), j % tall, 0)
        returned = total[PAD : PAD + width]
        center = field[l + 1, PAD : PAD + width]
        out[0, l] = mul[0, l] - ((1.0 - weight[...]) * center + returned)
        return carry

    lax.fori_loop(0, levels, one_level, 0)


def dual_final(mul, came_first, came, before, after, weight, up, lev):
    _, levels, width, rows = mul.shape
    vmem = pl.BlockSpec(memory_space=pltpu.VMEM)
    tall = width + 2 * PAD
    return pl.pallas_call(
        dual_kernel,
        in_specs=[vmem] * 8,
        out_specs=vmem,
        out_shape=jax.ShapeDtypeStruct((1, levels, width, rows), jnp.float32),
        scratch_shapes=[
            pltpu.VMEM((levels + 2, tall, rows), jnp.float32),
            pltpu.VMEM((tall, rows), jnp.float32),
            pltpu.VMEM((tall, rows), jnp.int32),
            pltpu.VMEM((tall, rows), jnp.int32),
        ],
        compiler_params=params(),
        cost_estimate=cost(1000, 1000),
    )(mul, came_first, came, before, after, weight, up, lev)


def per_device(
    increments,
    multipliers,
    departure_weight,
    upstream,
    level_offset,
    diffusivity,
    std_dev,
    vertical_inverse,
):
    columns = (departure_weight, upstream, level_offset)
    _, levels, width, rows = multipliers.shape
    inc_early, mul_early = (n * levels * width // 2048 for n in (LEAD, EARLY))
    inc_rows, mul_rows = increments.reshape(-1, rows), multipliers.reshape(-1, rows)
    inc_first = moved(inc_rows[:inc_early], 1, 0)
    mul_first = moved(mul_rows[:mul_early], -1, 0)
    to_right, to_left = pack(increments, multipliers, std_dev, diffusivity, *columns)
    before = moved(to_right, 0, 1)
    after = moved(to_left, 0, -1)
    inc_out, mul_out = forward(
        inc_early, mul_early, increments, multipliers, before, after
    )
    inc_rest = moved(inc_out, 1, 0)
    mul_rest = moved(mul_out, -1, 0)

    exact = dict(precision=lax.Precision.HIGHEST, preferred_element_type=jnp.float32)
    power = jnp.dot(vertical_inverse, vertical_inverse, **exact)
    power = jnp.dot(power, power, **exact)
    base = covar(multipliers, increments, std_dev, diffusivity, before, after, power)
    primal = primal_final(base, inc_first, inc_rest, *columns)
    weight, primal = lax.optimization_barrier((departure_weight, primal))
    dual = dual_final(
        multipliers, mul_first, mul_rest, before, after, weight, upstream, level_offset
    )
    return (primal, dual)


def solution(mesh):
    in_specs = (
        P("win", None, "tile", None),
        P("win", None, "tile", None),
        P("tile", None),
        P("tile", None),
        P("tile", None),
        P("tile", None),
        P("tile", None),
        P(),
    )
    out_specs = (P("win", None, "tile", None), P("win", None, "tile", None))
    return jax.shard_map(
        per_device, mesh=mesh, in_specs=in_specs, out_specs=out_specs, check_vma=False
    )
```

```python
import functools

import jax
import jax.numpy as jnp
from jax import lax
from jax.experimental import pallas as pl
from jax.experimental.pallas import tpu as pltpu
from jax.sharding import PartitionSpec as P

SWEEPS = 4
REACH = 2
PAD = 8
EARLY = 1080
LEAD = 1536
VMEM_LIMIT = 40 * 1024 * 1024
VMEM_WHOLE = 60 * 1024 * 1024


def moved(value, win_by, tile_by):
    wins, tiles = lax.axis_size("win"), lax.axis_size("tile")
    pairs = [
        (k * tiles + t, (k + win_by) * tiles + (t + tile_by) % tiles)
        for k in range(wins)
        for t in range(tiles)
        if 0 <= k + win_by < wins
    ]
    return lax.ppermute(value, ("win", "tile"), pairs)


def params():
    return pltpu.CompilerParams(vmem_limit_bytes=VMEM_LIMIT)


def cost(flops, touched):
    return pl.CostEstimate(flops=flops, bytes_accessed=touched, transcendentals=0)


class Rows:
    def __init__(self, levels):
        base = SWEEPS * levels
        self.std = slice(base, base + SWEEPS)
        self.kappa = slice(base + SWEEPS, base + 2 * SWEEPS)
        self.weight = slice(base + 2 * SWEEPS, base + 2 * SWEEPS + REACH)
        self.code = slice(base + 2 * SWEEPS + REACH, base + 2 * SWEEPS + 2 * REACH)
        self.fields = base + 4 * SWEEPS
        self.count = self.fields + REACH * levels

    def mul(self, l):
        return slice(SWEEPS * l, SWEEPS * (l + 1))

    def inc(self, l):
        return slice(self.fields + REACH * l, self.fields + REACH * (l + 1))


def pack_one(levels, refs, out, from_end):
    inc, mul, std, kappa, weight, up, lev = refs
    wide = slice(PAD - SWEEPS, PAD) if from_end else slice(0, SWEEPS)
    thin = slice(PAD - REACH, PAD) if from_end else slice(0, REACH)
    spot = Rows(levels)
    for l in range(levels):
        out[spot.mul(l)] = mul[0, l, wide]
        out[spot.inc(l)] = inc[0, l, thin]
    out[spot.std] = std[wide]
    out[spot.kappa] = kappa[wide]
    out[spot.weight] = weight[thin]
    out[spot.code] = up[thin].astype(jnp.float32) * 3.0 + lev[thin].astype(jnp.float32)
    gap = slice(spot.code.stop, spot.fields)
    out[gap] = jnp.zeros_like(out[gap])


def pack_both(levels, *refs):
    pack_one(levels, refs[0:7], refs[14], True)
    pack_one(levels, refs[7:14], refs[15], False)


def pack(inc, mul, std, kappa, weight, up, lev):
    _, levels, width, rows = mul.shape
    arrays = [inc, mul, std, kappa, weight, up, lev]
    specs = []
    for block in (width // PAD - 1, 0):
        for a in arrays:
            lead = a.shape[:-2]
            index = (0,) * len(lead) + (block, 0)
            specs.append(
                pl.BlockSpec((*lead, PAD, rows), functools.partial(lambda index, i: index, index))
            )
    height = Rows(levels).count
    return pl.pallas_call(
        functools.partial(pack_both, levels),
        grid=(1,),
        in_specs=specs,
        out_specs=[pl.BlockSpec((height, rows), lambda i: (0, 0))] * 2,
        out_shape=[jax.ShapeDtypeStruct((height, rows), jnp.float32)] * 2,
        compiler_params=pltpu.CompilerParams(vmem_limit_bytes=VMEM_WHOLE),
        cost_estimate=cost(1000, 1000),
    )(*(arrays * 2))


def forward_kernel(inc_early, mul_early, inc, mul, before, after, inc_out, mul_out):
    _, levels, width, rows = mul.shape
    spot = Rows(levels)
    half = REACH * levels
    for early, source, target in ((inc_early, inc, inc_out), (mul_early, mul, mul_out)):
        base = levels * width - early
        for l in range(levels):
            start = max(early - l * width, 0)
            if start < width:
                part = slice(l * width + start - early, (l + 1) * width - early)
                target[part] = source[0, l, start:]
            near = slice(base + REACH * l, base + REACH * (l + 1))
            far = slice(near.start + half, near.stop + half)
            if source is inc:
                target[near] = before[spot.inc(l)]
                target[far] = after[spot.inc(l)]
            else:
                first, last = before[spot.mul(l)], after[spot.mul(l)]
                target[near] = first[SWEEPS - REACH :]
                target[far] = last[:REACH]


def forward(inc_early, mul_early, inc, mul, before, after):
    _, levels, width, rows = mul.shape
    vmem = pl.BlockSpec(memory_space=pltpu.VMEM)
    heights = [levels * width - early + 2 * REACH * levels for early in (inc_early, mul_early)]
    return pl.pallas_call(
        functools.partial(forward_kernel, inc_early, mul_early),
        in_specs=[vmem] * 4,
        out_specs=[vmem] * 2,
        out_shape=[jax.ShapeDtypeStruct((h, rows), jnp.float32) for h in heights],
        compiler_params=params(),
        cost_estimate=cost(1000, 1000),
    )(inc, mul, before, after)


def covar_kernel(
    mul, inc, std, kappa, before, after, power, out, kappa_ext, field, smooth
):
    levels, width, rows = smooth.shape
    tall = width + 2 * PAD
    spot = Rows(levels)
    kappa_ext[...] = jnp.zeros_like(kappa_ext)
    field[...] = jnp.zeros_like(field)
    kappa_ext[PAD : PAD + width] = kappa[...]
    kappa_ext[PAD - SWEEPS : PAD] = before[spot.kappa]
    kappa_ext[PAD + width : PAD + width + SWEEPS] = after[spot.kappa]
    for l in range(levels):
        field[l, PAD - SWEEPS : PAD] = before[spot.std] * before[spot.mul(l)]
        field[l, PAD + width : PAD + width + SWEEPS] = after[spot.std] * after[spot.mul(l)]
    lane = lax.broadcasted_iota(jnp.int32, (tall, rows), 1)
    first, last = lane == 0, lane == rows - 1

    def one_level(l, carry):
        field[l, PAD : PAD + width] = std[...] * mul[0, l]
        value = field[l]
        for _ in range(SWEEPS):
            north = jnp.where(last, 0.0, pltpu.roll(value, rows - 1, 1))
            south = jnp.where(first, 0.0, pltpu.roll(value, 1, 1))
            around = pltpu.roll(value, 1, 0) + pltpu.roll(value, tall - 1, 0)
            value = value + kappa_ext[...] * ((around + (north + south)) - 4.0 * value)
        smooth[l] = value[PAD : PAD + width]
        return carry

    lax.fori_loop(0, levels, one_level, 0)
    step = 2 * PAD

    def one_block(b, carry):
        part = pl.ds(pl.multiple_of(b * step, step), step)
        fields = [smooth[m, part] for m in range(levels)]
        scale = std[part]
        for l in range(levels):
            total = power[l, 0] * fields[0]
            for m in range(1, levels):
                total = total + power[l, m] * fields[m]
            out[l, part] = scale * total + inc[0, l, part]
        return carry

    lax.fori_loop(0, width // step, one_block, 0)


def covar(mul, inc, std, kappa, before, after, power):
    _, levels, width, rows = mul.shape
    vmem = pl.BlockSpec(memory_space=pltpu.VMEM)
    return pl.pallas_call(
        covar_kernel,
        in_specs=[vmem] * 6 + [pl.BlockSpec(memory_space=pltpu.SMEM)],
        out_specs=vmem,
        out_shape=jax.ShapeDtypeStruct((levels, width, rows), jnp.float32),
        scratch_shapes=[
            pltpu.VMEM((width + 2 * PAD, rows), jnp.float32),
            pltpu.VMEM((levels, width + 2 * PAD, rows), jnp.float32),
            pltpu.VMEM((levels, width, rows), jnp.float32),
        ],
        compiler_params=params(),
        cost_estimate=cost(1000, 1000),
    )(mul, inc, std, kappa, before, after, power)


def fill_field(field, offset, width, *pieces):
    levels = field.shape[0] - 2 * offset
    rest, half = pieces[-1], REACH * levels
    base = rest.shape[0] - 2 * half
    start = 0
    for piece in pieces:
        stop = start + (base if piece is rest else piece.shape[0])
        for l in range(levels):
            begin, end = max(l * width, start), min((l + 1) * width, stop)
            if begin < end:
                part = slice(PAD + begin - l * width, PAD + end - l * width)
                field[l + offset, part] = piece[begin - start : end - start]
        start = stop
    for l in range(levels):
        near = slice(base + REACH * l, base + REACH * (l + 1))
        field[l + offset, PAD - REACH : PAD] = rest[near]
        far = rest[near.start + half : near.stop + half]
        field[l + offset, PAD + width : PAD + width + REACH] = far


def primal_kernel(base, came_first, came, weight, up, lev, out, field, level_field):
    levels, width, rows = base.shape
    fill_field(field, 0, width, came_first, came)
    zero = jnp.zeros((width, rows), jnp.float32)
    level_field[0] = zero
    level_field[levels + 1] = zero

    def one_level(l, carry):
        step = up[...]
        total = field[l, PAD : PAD + width]
        for j in (-2, -1, 1, 2):
            total = jnp.where(step == j, field[l, PAD + j : PAD + j + width], total)
        level_field[l + 1] = total
        return carry

    lax.fori_loop(0, levels, one_level, 0)

    def combine(l, carry):
        pick = lev[...]
        departed = jnp.where(
            pick == 0,
            level_field[l + 1],
            jnp.where(pick == 1, level_field[l + 2], level_field[l]),
        )
        center = field[l, PAD : PAD + width]
        out[0, l] = base[l] - ((1.0 - weight[...]) * center + weight[...] * departed)
        return carry

    lax.fori_loop(0, levels, combine, 0)


def primal_final(base, came_first, came, weight, up, lev):
    levels, width, rows = base.shape
    vmem = pl.BlockSpec(memory_space=pltpu.VMEM)
    return pl.pallas_call(
        primal_kernel,
        in_specs=[vmem] * 6,
        out_specs=vmem,
        out_shape=jax.ShapeDtypeStruct((1, levels, width, rows), jnp.float32),
        scratch_shapes=[
            pltpu.VMEM((levels, width + 2 * PAD, rows), jnp.float32),
            pltpu.VMEM((levels + 2, width, rows), jnp.float32),
        ],
        compiler_params=params(),
        cost_estimate=cost(1000, 1000),
    )(base, came_first, came, weight, up, lev)


def dual_kernel(
    mul, came_first, came, before, after, weight, up, lev, out, field, weight_ext, up_ext, lev_ext
):
    _, levels, width, rows = mul.shape
    tall = width + 2 * PAD
    spot = Rows(levels)
    left, right = slice(PAD - REACH, PAD), slice(PAD + width, PAD + width + REACH)
    weight_ext[...] = jnp.zeros_like(weight_ext)
    up_ext[...] = jnp.zeros_like(up_ext)
    lev_ext[...] = jnp.zeros_like(lev_ext)
    weight_ext[PAD : PAD + width] = weight[...]
    up_ext[PAD : PAD + width] = up[...]
    lev_ext[PAD : PAD + width] = lev[...]
    zero = jnp.zeros((tall, rows), jnp.float32)
    field[0] = zero
    field[levels + 1] = zero
    for side, part in ((before, left), (after, right)):
        weight_ext[part] = side[spot.weight]
        code = side[spot.code]
        step = jnp.floor((code + 1.5) * (1.0 / 3.0))
        up_ext[part] = step.astype(jnp.int32)
        lev_ext[part] = (code - 3.0 * step).astype(jnp.int32)
    for l in range(levels):
        field[l + 1, :PAD] = zero[:PAD]
        field[l + 1, PAD + width :] = zero[:PAD]
    fill_field(field, 1, width, came_first, came)

    def one_level(l, carry):
        pick = lev_ext[...]
        lifted = jnp.where(
            pick == 0, field[l + 1], jnp.where(pick == 1, field[l], field[l + 2])
        )
        source = weight_ext[...] * lifted
        step = up_ext[...]
        total = jnp.where(step == 0, source, 0.0)
        for j in (-2, -1, 1, 2):
            total = total + pltpu.roll(jnp.where(step == j, source, 0.0), j % tall, 0)
        returned = total[PAD : PAD + width]
        center = field[l + 1, PAD : PAD + width]
        out[0, l] = mul[0, l] - ((1.0 - weight[...]) * center + returned)
        return carry

    lax.fori_loop(0, levels, one_level, 0)


def dual_final(mul, came_first, came, before, after, weight, up, lev):
    _, levels, width, rows = mul.shape
    vmem = pl.BlockSpec(memory_space=pltpu.VMEM)
    tall = width + 2 * PAD
    return pl.pallas_call(
        dual_kernel,
        in_specs=[vmem] * 8,
        out_specs=vmem,
        out_shape=jax.ShapeDtypeStruct((1, levels, width, rows), jnp.float32),
        scratch_shapes=[
            pltpu.VMEM((levels + 2, tall, rows), jnp.float32),
            pltpu.VMEM((tall, rows), jnp.float32),
            pltpu.VMEM((tall, rows), jnp.int32),
            pltpu.VMEM((tall, rows), jnp.int32),
        ],
        compiler_params=params(),
        cost_estimate=cost(1000, 1000),
    )(mul, came_first, came, before, after, weight, up, lev)


def per_device(
    increments,
    multipliers,
    departure_weight,
    upstream,
    level_offset,
    diffusivity,
    std_dev,
    vertical_inverse,
):
    columns = (departure_weight, upstream, level_offset)
    _, levels, width, rows = multipliers.shape
    inc_early, mul_early = (n * levels * width // 2048 for n in (LEAD, EARLY))
    inc_rows, mul_rows = increments.reshape(-1, rows), multipliers.reshape(-1, rows)
    inc_first = moved(inc_rows[:inc_early], 1, 0)
    mul_first = moved(mul_rows[:mul_early], -1, 0)
    to_right, to_left = pack(increments, multipliers, std_dev, diffusivity, *columns)
    before = moved(to_right, 0, 1)
    after = moved(to_left, 0, -1)
    inc_out, mul_out = forward(
        inc_early, mul_early, increments, multipliers, before, after
    )
    inc_rest = moved(inc_out, 1, 0)
    mul_rest = moved(mul_out, -1, 0)

    exact = dict(precision=lax.Precision.HIGHEST, preferred_element_type=jnp.float32)
    power = jnp.dot(vertical_inverse, vertical_inverse, **exact)
    power = jnp.dot(power, power, **exact)
    base = covar(multipliers, increments, std_dev, diffusivity, before, after, power)
    dual = dual_final(multipliers, mul_first, mul_rest, before, after, *columns)
    weight, dual = lax.optimization_barrier((departure_weight, dual))
    primal = primal_final(base, inc_first, inc_rest, weight, upstream, level_offset)
    return (primal, dual)


def solution(mesh):
    in_specs = (
        P("win", None, "tile", None),
        P("win", None, "tile", None),
        P("tile", None),
        P("tile", None),
        P("tile", None),
        P("tile", None),
        P("tile", None),
        P(),
    )
    out_specs = (P("win", None, "tile", None), P("win", None, "tile", None))
    return jax.shard_map(
        per_device, mesh=mesh, in_specs=in_specs, out_specs=out_specs, check_vma=False
    )
```

```python
import functools

import jax
import jax.numpy as jnp
from jax import lax
from jax.experimental import pallas as pl
from jax.experimental.pallas import tpu as pltpu
from jax.sharding import PartitionSpec as P

SWEEPS = 4
REACH = 2
PAD = 8
NEAR = 1408
FAR = 1088
GROUPS = 4
VMEM_LIMIT = 40 * 1024 * 1024
VMEM_WHOLE = 60 * 1024 * 1024


def shift_tile(value, by):
    tiles = lax.axis_size("tile")
    return lax.ppermute(value, "tile", [(t, (t + by) % tiles) for t in range(tiles)])


def swap_in_pair(value):
    wins = lax.axis_size("win")
    return lax.ppermute(value, "win", [(k, k ^ 1) for k in range(wins)])


def across_pairs(value):
    wins = lax.axis_size("win")
    pairs = [(k, k - 1 if k % 2 == 0 else k + 1) for k in range(1, wins - 1)]
    return lax.ppermute(value, "win", pairs)


def on_even(body_even, body_odd):
    odd = lax.rem(lax.axis_index("win"), 2)
    pl.when(odd == 0)(body_even)
    pl.when(odd == 1)(body_odd)


def params():
    return pltpu.CompilerParams(vmem_limit_bytes=VMEM_LIMIT)


def cost(flops, touched):
    return pl.CostEstimate(flops=flops, bytes_accessed=touched, transcendentals=0)


class Rows:
    def __init__(self, levels):
        base = SWEEPS * levels
        self.std = slice(base, base + SWEEPS)
        self.kappa = slice(base + SWEEPS, base + 2 * SWEEPS)
        self.weight = slice(base + 2 * SWEEPS, base + 2 * SWEEPS + REACH)
        self.code = slice(base + 2 * SWEEPS + REACH, base + 2 * SWEEPS + 2 * REACH)
        self.fields = base + 4 * SWEEPS
        self.count = self.fields + REACH * levels

    def mul(self, l):
        return slice(SWEEPS * l, SWEEPS * (l + 1))

    def inc(self, l):
        return slice(self.fields + REACH * l, self.fields + REACH * (l + 1))


def pack_one(levels, refs, out, from_end):
    inc, mul, std, kappa, weight, up, lev = refs
    wide = slice(PAD - SWEEPS, PAD) if from_end else slice(0, SWEEPS)
    thin = slice(PAD - REACH, PAD) if from_end else slice(0, REACH)
    spot = Rows(levels)
    for l in range(levels):
        out[spot.mul(l)] = mul[0, l, wide]
        out[spot.inc(l)] = inc[0, l, thin]
    out[spot.std] = std[wide]
    out[spot.kappa] = kappa[wide]
    out[spot.weight] = weight[thin]
    out[spot.code] = up[thin].astype(jnp.float32) * 3.0 + lev[thin].astype(jnp.float32)
    gap = slice(spot.code.stop, spot.fields)
    out[gap] = jnp.zeros_like(out[gap])


def pack_both(levels, *refs):
    pack_one(levels, refs[0:7], refs[14], True)
    pack_one(levels, refs[7:14], refs[15], False)


def pack(inc, mul, std, kappa, weight, up, lev):
    _, levels, width, rows = mul.shape
    arrays = [inc, mul, std, kappa, weight, up, lev]
    specs = []
    for block in (width // PAD - 1, 0):
        for a in arrays:
            lead = a.shape[:-2]
            index = (0,) * len(lead) + (block, 0)
            specs.append(
                pl.BlockSpec((*lead, PAD, rows), functools.partial(lambda index, i: index, index))
            )
    height = Rows(levels).count
    return pl.pallas_call(
        functools.partial(pack_both, levels),
        grid=(1,),
        in_specs=specs,
        out_specs=[pl.BlockSpec((height, rows), lambda i: (0, 0))] * 2,
        out_shape=[jax.ShapeDtypeStruct((height, rows), jnp.float32)] * 2,
        compiler_params=pltpu.CompilerParams(vmem_limit_bytes=VMEM_WHOLE),
        cost_estimate=cost(1000, 1000),
    )(*(arrays * 2))


def pick_kernel(even_source, odd_source, out, sems):
    size = out.shape[0] // GROUPS

    def copy(source):
        parts = [pl.ds(g * size, size) for g in range(GROUPS)]
        copies = [
            pltpu.make_async_copy(source.at[part], out.at[part], sems.at[g])
            for g, part in enumerate(parts)
        ]
        for moving in copies:
            moving.start()
        for moving in copies:
            moving.wait()

    on_even(lambda: copy(even_source), lambda: copy(odd_source))


def pick(even_source, odd_source, count):
    return pl.pallas_call(
        pick_kernel,
        in_specs=[pl.BlockSpec(memory_space=pl.ANY)] * 2,
        out_specs=pl.BlockSpec(memory_space=pltpu.VMEM),
        out_shape=jax.ShapeDtypeStruct((count, even_source.shape[1]), jnp.float32),
        scratch_shapes=[pltpu.SemaphoreType.DMA((GROUPS,))],
        compiler_params=pltpu.CompilerParams(vmem_limit_bytes=VMEM_WHOLE),
        cost_estimate=cost(1000, 1000),
    )(even_source, odd_source)


def forward_kernel(near_early, far_early, inc, mul, before, after, near_out, far_out):
    _, levels, width, rows = mul.shape
    spot = Rows(levels)
    half = REACH * levels

    def copy(early, source, target):
        base = levels * width - early
        for l in range(levels):
            start = max(early - l * width, 0)
            if start < width:
                part = slice(l * width + start - early, (l + 1) * width - early)
                target[part] = source[0, l, start:]
            left = slice(base + REACH * l, base + REACH * (l + 1))
            right = slice(left.start + half, left.stop + half)
            if source is inc:
                target[left] = before[spot.inc(l)]
                target[right] = after[spot.inc(l)]
            else:
                first, last = before[spot.mul(l)], after[spot.mul(l)]
                target[left] = first[SWEEPS - REACH :]
                target[right] = last[:REACH]

    def even():
        copy(near_early, inc, near_out)
        copy(far_early, mul, far_out)

    def odd():
        copy(near_early, mul, near_out)
        copy(far_early, inc, far_out)

    on_even(even, odd)


def forward(near_early, far_early, inc, mul, before, after):
    _, levels, width, rows = mul.shape
    vmem = pl.BlockSpec(memory_space=pltpu.VMEM)
    heights = [levels * width - early + 2 * REACH * levels for early in (near_early, far_early)]
    return pl.pallas_call(
        functools.partial(forward_kernel, near_early, far_early),
        in_specs=[vmem] * 4,
        out_specs=[vmem] * 2,
        out_shape=[jax.ShapeDtypeStruct((h, rows), jnp.float32) for h in heights],
        compiler_params=params(),
        cost_estimate=cost(1000, 1000),
    )(inc, mul, before, after)


def covar_kernel(
    mul, inc, std, kappa, before, after, power, out, kappa_ext, field, smooth
):
    levels, width, rows = smooth.shape
    tall = width + 2 * PAD
    spot = Rows(levels)
    kappa_ext[...] = jnp.zeros_like(kappa_ext)
    field[...] = jnp.zeros_like(field)
    kappa_ext[PAD : PAD + width] = kappa[...]
    kappa_ext[PAD - SWEEPS : PAD] = before[spot.kappa]
    kappa_ext[PAD + width : PAD + width + SWEEPS] = after[spot.kappa]
    for l in range(levels):
        field[l, PAD - SWEEPS : PAD] = before[spot.std] * before[spot.mul(l)]
        field[l, PAD + width : PAD + width + SWEEPS] = after[spot.std] * after[spot.mul(l)]
    lane = lax.broadcasted_iota(jnp.int32, (tall, rows), 1)
    first, last = lane == 0, lane == rows - 1

    def one_level(l, carry):
        field[l, PAD : PAD + width] = std[...] * mul[0, l]
        value = field[l]
        for _ in range(SWEEPS):
            north = jnp.where(last, 0.0, pltpu.roll(value, rows - 1, 1))
            south = jnp.where(first, 0.0, pltpu.roll(value, 1, 1))
            around = pltpu.roll(value, 1, 0) + pltpu.roll(value, tall - 1, 0)
            value = value + kappa_ext[...] * ((around + (north + south)) - 4.0 * value)
        smooth[l] = value[PAD : PAD + width]
        return carry

    lax.fori_loop(0, levels, one_level, 0)
    step = 2 * PAD

    def one_block(b, carry):
        part = pl.ds(pl.multiple_of(b * step, step), step)
        fields = [smooth[m, part] for m in range(levels)]
        scale = std[part]
        for l in range(levels):
            total = power[l, 0] * fields[0]
            for m in range(1, levels):
                total = total + power[l, m] * fields[m]
            out[l, part] = scale * total + inc[0, l, part]
        return carry

    lax.fori_loop(0, width // step, one_block, 0)


def covar(mul, inc, std, kappa, before, after, power):
    _, levels, width, rows = mul.shape
    vmem = pl.BlockSpec(memory_space=pltpu.VMEM)
    return pl.pallas_call(
        covar_kernel,
        in_specs=[vmem] * 6 + [pl.BlockSpec(memory_space=pltpu.SMEM)],
        out_specs=vmem,
        out_shape=jax.ShapeDtypeStruct((levels, width, rows), jnp.float32),
        scratch_shapes=[
            pltpu.VMEM((width + 2 * PAD, rows), jnp.float32),
            pltpu.VMEM((levels, width + 2 * PAD, rows), jnp.float32),
            pltpu.VMEM((levels, width, rows), jnp.float32),
        ],
        compiler_params=params(),
        cost_estimate=cost(1000, 1000),
    )(mul, inc, std, kappa, before, after, power)


def fill_field(field, width, *pieces):
    levels = field.shape[0] - 2
    rest, half = pieces[-1], REACH * levels
    base = rest.shape[0] - 2 * half
    zero = jnp.zeros_like(field[0])
    field[0] = zero
    field[levels + 1] = zero
    start = 0
    for piece in pieces:
        stop = start + (base if piece is rest else piece.shape[0])
        for l in range(levels):
            begin, end = max(l * width, start), min((l + 1) * width, stop)
            if begin < end:
                part = slice(PAD + begin - l * width, PAD + end - l * width)
                field[l + 1, part] = piece[begin - start : end - start]
        start = stop
    for l in range(levels):
        near = slice(base + REACH * l, base + REACH * (l + 1))
        field[l + 1, :PAD] = zero[:PAD]
        field[l + 1, PAD + width :] = zero[:PAD]
        field[l + 1, PAD - REACH : PAD] = rest[near]
        far = rest[near.start + half : near.stop + half]
        field[l + 1, PAD + width : PAD + width + REACH] = far


def in_groups(levels, body, staged, out, sems):
    size = levels // GROUPS
    copies = []
    for g in range(GROUPS):
        lax.fori_loop(g * size, (g + 1) * size, lambda l, carry: body(l) or carry, 0)
        part = pl.ds(g * size, size)
        copy = pltpu.make_async_copy(staged.at[part], out.at[0, part], sems.at[g])
        copy.start()
        copies.append(copy)
    for copy in copies:
        copy.wait()


def primal_levels(base, weight, up, lev, field, level_field, staged, out, sems):
    levels, width, rows = base.shape
    zero = jnp.zeros((width, rows), jnp.float32)
    level_field[0] = zero
    level_field[levels + 1] = zero

    def one_level(l, carry):
        step = up[...]
        total = field[l + 1, PAD : PAD + width]
        for j in (-2, -1, 1, 2):
            total = jnp.where(step == j, field[l + 1, PAD + j : PAD + j + width], total)
        level_field[l + 1] = total
        return carry

    lax.fori_loop(0, levels, one_level, 0)

    def combine(l):
        pick = lev[...]
        departed = jnp.where(
            pick == 0,
            level_field[l + 1],
            jnp.where(pick == 1, level_field[l + 2], level_field[l]),
        )
        center = field[l + 1, PAD : PAD + width]
        staged[l] = base[l] - ((1.0 - weight[...]) * center + weight[...] * departed)

    in_groups(levels, combine, staged, out, sems)


def dual_levels(
    mul, before, after, weight, up, lev, field, weight_ext, up_ext, lev_ext, staged, out, sems
):
    _, levels, width, rows = mul.shape
    tall = width + 2 * PAD
    spot = Rows(levels)
    weight_ext[...] = jnp.zeros_like(weight_ext)
    up_ext[...] = jnp.zeros_like(up_ext)
    lev_ext[...] = jnp.zeros_like(lev_ext)
    weight_ext[PAD : PAD + width] = weight[...]
    up_ext[PAD : PAD + width] = up[...]
    lev_ext[PAD : PAD + width] = lev[...]
    left, right = slice(PAD - REACH, PAD), slice(PAD + width, PAD + width + REACH)
    for side, part in ((before, left), (after, right)):
        weight_ext[part] = side[spot.weight]
        code = side[spot.code]
        step = jnp.floor((code + 1.5) * (1.0 / 3.0))
        up_ext[part] = step.astype(jnp.int32)
        lev_ext[part] = (code - 3.0 * step).astype(jnp.int32)

    def one_level(l):
        pick = lev_ext[...]
        lifted = jnp.where(
            pick == 0, field[l + 1], jnp.where(pick == 1, field[l], field[l + 2])
        )
        source = weight_ext[...] * lifted
        step = up_ext[...]
        total = jnp.where(step == 0, source, 0.0)
        for j in (-2, -1, 1, 2):
            total = total + pltpu.roll(jnp.where(step == j, source, 0.0), j % tall, 0)
        returned = total[PAD : PAD + width]
        center = field[l + 1, PAD : PAD + width]
        staged[l] = mul[0, l] - ((1.0 - weight[...]) * center + returned)

    in_groups(levels, one_level, staged, out, sems)


def final_kernel(primal_on_even, last, base, mul, first, rest, before, after, weight, up, lev, *refs):
    if last:
        refs = refs[2:]
    primal, dual, field, level_field, weight_ext, up_ext, lev_ext, staged, sems = refs
    fill_field(field, mul.shape[2], first, rest)

    def make_primal():
        primal_levels(base, weight, up, lev, field, level_field, staged, primal, sems)

    def make_dual():
        dual_levels(
            mul, before, after, weight, up, lev, field, weight_ext, up_ext, lev_ext,
            staged, dual, sems,
        )

    if primal_on_even:
        on_even(make_primal, make_dual)
    else:
        on_even(make_dual, make_primal)


def final(primal_on_even, base, mul, pieces, before, after, columns, done=()):
    _, levels, width, rows = mul.shape
    vmem = pl.BlockSpec(memory_space=pltpu.VMEM)
    anywhere = pl.BlockSpec(memory_space=pl.ANY)
    tall = width + 2 * PAD
    return pl.pallas_call(
        functools.partial(final_kernel, primal_on_even, bool(done)),
        in_specs=[vmem] * 9 + [anywhere] * len(done),
        out_specs=[anywhere] * 2,
        out_shape=[jax.ShapeDtypeStruct(mul.shape, jnp.float32)] * 2,
        input_output_aliases={9: 0, 10: 1} if done else {},
        scratch_shapes=[
            pltpu.VMEM((levels + 2, tall, rows), jnp.float32),
            pltpu.VMEM((levels + 2, width, rows), jnp.float32),
            pltpu.VMEM((tall, rows), jnp.float32),
            pltpu.VMEM((tall, rows), jnp.int32),
            pltpu.VMEM((tall, rows), jnp.int32),
            pltpu.VMEM((levels, width, rows), jnp.float32),
            pltpu.SemaphoreType.DMA((GROUPS,)),
        ],
        compiler_params=params(),
        cost_estimate=cost(1000, 1000),
    )(base, mul, *pieces, before, after, *columns, *done)


def per_device(
    increments,
    multipliers,
    departure_weight,
    upstream,
    level_offset,
    diffusivity,
    std_dev,
    vertical_inverse,
):
    columns = (departure_weight, upstream, level_offset)
    _, levels, width, rows = multipliers.shape
    near_early, far_early = (n * levels * width // 2048 for n in (NEAR, FAR))
    inc_rows, mul_rows = increments.reshape(-1, rows), multipliers.reshape(-1, rows)
    near_first = swap_in_pair(pick(inc_rows, mul_rows, near_early))
    far_first = across_pairs(pick(mul_rows, inc_rows, far_early))
    to_right, to_left = pack(increments, multipliers, std_dev, diffusivity, *columns)
    before = shift_tile(to_right, 1)
    after = shift_tile(to_left, -1)
    near_out, far_out = forward(near_early, far_early, increments, multipliers, before, after)
    near_rest = swap_in_pair(near_out)
    far_rest = across_pairs(far_out)

    exact = dict(precision=lax.Precision.HIGHEST, preferred_element_type=jnp.float32)
    power = jnp.dot(vertical_inverse, vertical_inverse, **exact)
    power = jnp.dot(power, power, **exact)
    base = covar(multipliers, increments, std_dev, diffusivity, before, after, power)
    done = final(True, base, multipliers, (far_first, far_rest), before, after, columns)
    primal, dual = final(
        False, base, multipliers, (near_first, near_rest), before, after, columns, done
    )
    return (primal, dual)


def solution(mesh):
    in_specs = (
        P("win", None, "tile", None),
        P("win", None, "tile", None),
        P("tile", None),
        P("tile", None),
        P("tile", None),
        P("tile", None),
        P("tile", None),
        P(),
    )
    out_specs = (P("win", None, "tile", None), P("win", None, "tile", None))
    return jax.shard_map(
        per_device, mesh=mesh, in_specs=in_specs, out_specs=out_specs, check_vma=False
    )
```

```python
import functools

import jax
import jax.numpy as jnp
from jax import lax
from jax.experimental import pallas as pl
from jax.experimental.pallas import tpu as pltpu
from jax.sharding import PartitionSpec as P

SWEEPS = 4
REACH = 2
PAD = 8
NEAR = 1408
FAR = 1088
GROUPS = 4
VMEM_LIMIT = 40 * 1024 * 1024
VMEM_WHOLE = 60 * 1024 * 1024


def shift_tile(value, by):
    tiles = lax.axis_size("tile")
    return lax.ppermute(value, "tile", [(t, (t + by) % tiles) for t in range(tiles)])


def swap_in_pair(value):
    wins = lax.axis_size("win")
    return lax.ppermute(value, "win", [(k, k ^ 1) for k in range(wins)])


def across_pairs(value):
    wins = lax.axis_size("win")
    pairs = [(k, k - 1 if k % 2 == 0 else k + 1) for k in range(1, wins - 1)]
    return lax.ppermute(value, "win", pairs)


def on_even(body_even, body_odd):
    odd = lax.rem(lax.axis_index("win"), 2)
    pl.when(odd == 0)(body_even)
    pl.when(odd == 1)(body_odd)


def params():
    return pltpu.CompilerParams(vmem_limit_bytes=VMEM_LIMIT)


def cost(flops, touched):
    return pl.CostEstimate(flops=flops, bytes_accessed=touched, transcendentals=0)


class Rows:
    def __init__(self, levels):
        base = SWEEPS * levels
        self.std = slice(base, base + SWEEPS)
        self.kappa = slice(base + SWEEPS, base + 2 * SWEEPS)
        self.weight = slice(base + 2 * SWEEPS, base + 2 * SWEEPS + REACH)
        self.code = slice(base + 2 * SWEEPS + REACH, base + 2 * SWEEPS + 2 * REACH)
        self.fields = base + 4 * SWEEPS
        self.count = self.fields + REACH * levels

    def mul(self, l):
        return slice(SWEEPS * l, SWEEPS * (l + 1))

    def inc(self, l):
        return slice(self.fields + REACH * l, self.fields + REACH * (l + 1))


def pack_one(levels, refs, out, from_end):
    inc, mul, std, kappa, weight, up, lev = refs
    wide = slice(PAD - SWEEPS, PAD) if from_end else slice(0, SWEEPS)
    thin = slice(PAD - REACH, PAD) if from_end else slice(0, REACH)
    spot = Rows(levels)
    for l in range(levels):
        out[spot.mul(l)] = mul[0, l, wide]
        out[spot.inc(l)] = inc[0, l, thin]
    out[spot.std] = std[wide]
    out[spot.kappa] = kappa[wide]
    out[spot.weight] = weight[thin]
    out[spot.code] = up[thin].astype(jnp.float32) * 3.0 + lev[thin].astype(jnp.float32)
    gap = slice(spot.code.stop, spot.fields)
    out[gap] = jnp.zeros_like(out[gap])


def pack_both(levels, *refs):
    pack_one(levels, refs[0:7], refs[14], True)
    pack_one(levels, refs[7:14], refs[15], False)


def pack(inc, mul, std, kappa, weight, up, lev):
    _, levels, width, rows = mul.shape
    arrays = [inc, mul, std, kappa, weight, up, lev]
    specs = []
    for block in (width // PAD - 1, 0):
        for a in arrays:
            lead = a.shape[:-2]
            index = (0,) * len(lead) + (block, 0)
            specs.append(
                pl.BlockSpec((*lead, PAD, rows), functools.partial(lambda index, i: index, index))
            )
    height = Rows(levels).count
    return pl.pallas_call(
        functools.partial(pack_both, levels),
        grid=(1,),
        in_specs=specs,
        out_specs=[pl.BlockSpec((height, rows), lambda i: (0, 0))] * 2,
        out_shape=[jax.ShapeDtypeStruct((height, rows), jnp.float32)] * 2,
        compiler_params=pltpu.CompilerParams(vmem_limit_bytes=VMEM_WHOLE),
        cost_estimate=cost(1000, 1000),
    )(*(arrays * 2))


def pick_kernel(even_source, odd_source, out, sems):
    size = out.shape[0] // GROUPS

    def copy(source):
        parts = [pl.ds(g * size, size) for g in range(GROUPS)]
        copies = [
            pltpu.make_async_copy(source.at[part], out.at[part], sems.at[g])
            for g, part in enumerate(parts)
        ]
        for moving in copies:
            moving.start()
        for moving in copies:
            moving.wait()

    on_even(lambda: copy(even_source), lambda: copy(odd_source))


def pick(even_source, odd_source, count):
    return pl.pallas_call(
        pick_kernel,
        in_specs=[pl.BlockSpec(memory_space=pl.ANY)] * 2,
        out_specs=pl.BlockSpec(memory_space=pltpu.VMEM),
        out_shape=jax.ShapeDtypeStruct((count, even_source.shape[1]), jnp.float32),
        scratch_shapes=[pltpu.SemaphoreType.DMA((GROUPS,))],
        compiler_params=pltpu.CompilerParams(vmem_limit_bytes=VMEM_WHOLE),
        cost_estimate=cost(1000, 1000),
    )(even_source, odd_source)


def forward_kernel(near_early, far_early, inc, mul, before, after, near_out, far_out):
    _, levels, width, rows = mul.shape
    spot = Rows(levels)
    half = REACH * levels

    def copy(early, source, target):
        base = levels * width - early
        for l in range(levels):
            start = max(early - l * width, 0)
            if start < width:
                part = slice(l * width + start - early, (l + 1) * width - early)
                target[part] = source[0, l, start:]
            left = slice(base + REACH * l, base + REACH * (l + 1))
            right = slice(left.start + half, left.stop + half)
            if source is inc:
                target[left] = before[spot.inc(l)]
                target[right] = after[spot.inc(l)]
            else:
                first, last = before[spot.mul(l)], after[spot.mul(l)]
                target[left] = first[SWEEPS - REACH :]
                target[right] = last[:REACH]

    def even():
        copy(near_early, inc, near_out)
        copy(far_early, mul, far_out)

    def odd():
        copy(near_early, mul, near_out)
        copy(far_early, inc, far_out)

    on_even(even, odd)


def forward(near_early, far_early, inc, mul, before, after):
    _, levels, width, rows = mul.shape
    vmem = pl.BlockSpec(memory_space=pltpu.VMEM)
    heights = [levels * width - early + 2 * REACH * levels for early in (near_early, far_early)]
    return pl.pallas_call(
        functools.partial(forward_kernel, near_early, far_early),
        in_specs=[vmem] * 4,
        out_specs=[vmem] * 2,
        out_shape=[jax.ShapeDtypeStruct((h, rows), jnp.float32) for h in heights],
        compiler_params=params(),
        cost_estimate=cost(1000, 1000),
    )(inc, mul, before, after)


def covar_kernel(
    mul, inc, std, kappa, before, after, power, out, kappa_ext, field, smooth
):
    levels, width, rows = smooth.shape
    tall = width + 2 * PAD
    spot = Rows(levels)
    kappa_ext[...] = jnp.zeros_like(kappa_ext)
    field[...] = jnp.zeros_like(field)
    kappa_ext[PAD : PAD + width] = kappa[...]
    kappa_ext[PAD - SWEEPS : PAD] = before[spot.kappa]
    kappa_ext[PAD + width : PAD + width + SWEEPS] = after[spot.kappa]
    for l in range(levels):
        field[l, PAD - SWEEPS : PAD] = before[spot.std] * before[spot.mul(l)]
        field[l, PAD + width : PAD + width + SWEEPS] = after[spot.std] * after[spot.mul(l)]
    lane = lax.broadcasted_iota(jnp.int32, (tall, rows), 1)
    first, last = lane == 0, lane == rows - 1

    def one_level(l, carry):
        field[l, PAD : PAD + width] = std[...] * mul[0, l]
        value = field[l]
        for _ in range(SWEEPS):
            north = jnp.where(last, 0.0, pltpu.roll(value, rows - 1, 1))
            south = jnp.where(first, 0.0, pltpu.roll(value, 1, 1))
            around = pltpu.roll(value, 1, 0) + pltpu.roll(value, tall - 1, 0)
            value = value + kappa_ext[...] * ((around + (north + south)) - 4.0 * value)
        smooth[l] = value[PAD : PAD + width]
        return carry

    lax.fori_loop(0, levels, one_level, 0)
    step = 2 * PAD

    def one_block(b, carry):
        part = pl.ds(pl.multiple_of(b * step, step), step)
        fields = [smooth[m, part] for m in range(levels)]
        scale = std[part]
        for l in range(levels):
            total = power[l, 0] * fields[0]
            for m in range(1, levels):
                total = total + power[l, m] * fields[m]
            out[l, part] = scale * total + inc[0, l, part]
        return carry

    lax.fori_loop(0, width // step, one_block, 0)


def covar(mul, inc, std, kappa, before, after, power):
    _, levels, width, rows = mul.shape
    vmem = pl.BlockSpec(memory_space=pltpu.VMEM)
    return pl.pallas_call(
        covar_kernel,
        in_specs=[vmem] * 6 + [pl.BlockSpec(memory_space=pltpu.SMEM)],
        out_specs=vmem,
        out_shape=jax.ShapeDtypeStruct((levels, width, rows), jnp.float32),
        scratch_shapes=[
            pltpu.VMEM((width + 2 * PAD, rows), jnp.float32),
            pltpu.VMEM((levels, width + 2 * PAD, rows), jnp.float32),
            pltpu.VMEM((levels, width, rows), jnp.float32),
        ],
        compiler_params=params(),
        cost_estimate=cost(1000, 1000),
    )(mul, inc, std, kappa, before, after, power)


def fill_field(field, width, *pieces):
    levels = field.shape[0] - 2
    rest, half = pieces[-1], REACH * levels
    base = rest.shape[0] - 2 * half
    zero = jnp.zeros_like(field[0])
    field[0] = zero
    field[levels + 1] = zero
    start = 0
    for piece in pieces:
        stop = start + (base if piece is rest else piece.shape[0])
        for l in range(levels):
            begin, end = max(l * width, start), min((l + 1) * width, stop)
            if begin < end:
                part = slice(PAD + begin - l * width, PAD + end - l * width)
                field[l + 1, part] = piece[begin - start : end - start]
        start = stop
    for l in range(levels):
        near = slice(base + REACH * l, base + REACH * (l + 1))
        field[l + 1, :PAD] = zero[:PAD]
        field[l + 1, PAD + width :] = zero[:PAD]
        field[l + 1, PAD - REACH : PAD] = rest[near]
        far = rest[near.start + half : near.stop + half]
        field[l + 1, PAD + width : PAD + width + REACH] = far


def in_groups(levels, body, staged, out, sems):
    size = levels // GROUPS
    copies = []
    for g in range(GROUPS):
        lax.fori_loop(g * size, (g + 1) * size, lambda l, carry: body(l) or carry, 0)
        part = pl.ds(g * size, size)
        copy = pltpu.make_async_copy(staged.at[part], out.at[0, part], sems.at[g])
        copy.start()
        copies.append(copy)
    for copy in copies:
        copy.wait()


def primal_levels(base, weight, up, lev, field, level_field, staged, out, sems):
    levels, width, rows = base.shape
    zero = jnp.zeros((width, rows), jnp.float32)
    level_field[0] = zero
    level_field[levels + 1] = zero

    def one_level(l, carry):
        step = up[...]
        total = field[l + 1, PAD : PAD + width]
        for j in (-2, -1, 1, 2):
            total = jnp.where(step == j, field[l + 1, PAD + j : PAD + j + width], total)
        level_field[l + 1] = total
        return carry

    lax.fori_loop(0, levels, one_level, 0)

    def combine(l):
        pick = lev[...]
        departed = jnp.where(
            pick == 0,
            level_field[l + 1],
            jnp.where(pick == 1, level_field[l + 2], level_field[l]),
        )
        center = field[l + 1, PAD : PAD + width]
        staged[l] = base[l] - ((1.0 - weight[...]) * center + weight[...] * departed)

    in_groups(levels, combine, staged, out, sems)


def dual_levels(
    mul, before, after, weight, up, lev, field, weight_ext, up_ext, lev_ext, staged, out, sems
):
    _, levels, width, rows = mul.shape
    tall = width + 2 * PAD
    spot = Rows(levels)
    weight_ext[...] = jnp.zeros_like(weight_ext)
    up_ext[...] = jnp.zeros_like(up_ext)
    lev_ext[...] = jnp.zeros_like(lev_ext)
    weight_ext[PAD : PAD + width] = weight[...]
    up_ext[PAD : PAD + width] = up[...]
    lev_ext[PAD : PAD + width] = lev[...]
    left, right = slice(PAD - REACH, PAD), slice(PAD + width, PAD + width + REACH)
    for side, part in ((before, left), (after, right)):
        weight_ext[part] = side[spot.weight]
        code = side[spot.code]
        step = jnp.floor((code + 1.5) * (1.0 / 3.0))
        up_ext[part] = step.astype(jnp.int32)
        lev_ext[part] = (code - 3.0 * step).astype(jnp.int32)

    def one_level(l):
        pick = lev_ext[...]
        lifted = jnp.where(
            pick == 0, field[l + 1], jnp.where(pick == 1, field[l], field[l + 2])
        )
        source = weight_ext[...] * lifted
        step = up_ext[...]
        total = jnp.where(step == 0, source, 0.0)
        for j in (-2, -1, 1, 2):
            total = total + pltpu.roll(jnp.where(step == j, source, 0.0), j % tall, 0)
        returned = total[PAD : PAD + width]
        center = field[l + 1, PAD : PAD + width]
        staged[l] = mul[0, l] - ((1.0 - weight[...]) * center + returned)

    in_groups(levels, one_level, staged, out, sems)


def final_kernel(primal_on_even, last, base, mul, first, rest, before, after, weight, up, lev, *refs):
    if last:
        refs = refs[2:]
    primal, dual, field, level_field, weight_ext, up_ext, lev_ext, staged, sems = refs
    fill_field(field, mul.shape[2], first, rest)

    def make_primal():
        primal_levels(base, weight, up, lev, field, level_field, staged, primal, sems)

    def make_dual():
        dual_levels(
            mul, before, after, weight, up, lev, field, weight_ext, up_ext, lev_ext,
            staged, dual, sems,
        )

    if primal_on_even:
        on_even(make_primal, make_dual)
    else:
        on_even(make_dual, make_primal)


def final(primal_on_even, base, mul, pieces, before, after, columns, done=()):
    _, levels, width, rows = mul.shape
    vmem = pl.BlockSpec(memory_space=pltpu.VMEM)
    anywhere = pl.BlockSpec(memory_space=pl.ANY)
    tall = width + 2 * PAD
    return pl.pallas_call(
        functools.partial(final_kernel, primal_on_even, bool(done)),
        in_specs=[vmem] * 9 + [anywhere] * len(done),
        out_specs=[anywhere] * 2,
        out_shape=[jax.ShapeDtypeStruct(mul.shape, jnp.float32)] * 2,
        input_output_aliases={9: 0, 10: 1} if done else {},
        scratch_shapes=[
            pltpu.VMEM((levels + 2, tall, rows), jnp.float32),
            pltpu.VMEM((levels + 2, width, rows), jnp.float32),
            pltpu.VMEM((tall, rows), jnp.float32),
            pltpu.VMEM((tall, rows), jnp.int32),
            pltpu.VMEM((tall, rows), jnp.int32),
            pltpu.VMEM((levels, width, rows), jnp.float32),
            pltpu.SemaphoreType.DMA((GROUPS,)),
        ],
        compiler_params=params(),
        cost_estimate=cost(1000, 1000),
    )(base, mul, *pieces, before, after, *columns, *done)


def per_device(
    increments,
    multipliers,
    departure_weight,
    upstream,
    level_offset,
    diffusivity,
    std_dev,
    vertical_inverse,
):
    columns = (departure_weight, upstream, level_offset)
    _, levels, width, rows = multipliers.shape
    near_early, far_early = (n * levels * width // 2048 for n in (NEAR, FAR))
    inc_rows, mul_rows = increments.reshape(-1, rows), multipliers.reshape(-1, rows)
    even = lax.rem(lax.axis_index("win"), 2) == 0
    near_part = jnp.where(even, inc_rows[:near_early], mul_rows[:near_early])
    near_first = swap_in_pair(near_part)
    far_first = across_pairs(pick(mul_rows, inc_rows, far_early))
    to_right, to_left = pack(increments, multipliers, std_dev, diffusivity, *columns)
    before = shift_tile(to_right, 1)
    after = shift_tile(to_left, -1)
    near_out, far_out = forward(near_early, far_early, increments, multipliers, before, after)
    near_rest = swap_in_pair(near_out)
    far_rest = across_pairs(far_out)

    exact = dict(precision=lax.Precision.HIGHEST, preferred_element_type=jnp.float32)
    power = jnp.dot(vertical_inverse, vertical_inverse, **exact)
    power = jnp.dot(power, power, **exact)
    base = covar(multipliers, increments, std_dev, diffusivity, before, after, power)
    done = final(True, base, multipliers, (far_first, far_rest), before, after, columns)
    primal, dual = final(
        False, base, multipliers, (near_first, near_rest), before, after, columns, done
    )
    return (primal, dual)


def solution(mesh):
    in_specs = (
        P("win", None, "tile", None),
        P("win", None, "tile", None),
        P("tile", None),
        P("tile", None),
        P("tile", None),
        P("tile", None),
        P("tile", None),
        P(),
    )
    out_specs = (P("win", None, "tile", None), P("win", None, "tile", None))
    return jax.shard_map(
        per_device, mesh=mesh, in_specs=in_specs, out_specs=out_specs, check_vma=False
    )
```

```python
import functools

import jax
import jax.numpy as jnp
from jax import lax
from jax.experimental import pallas as pl
from jax.experimental.pallas import tpu as pltpu
from jax.sharding import PartitionSpec as P

SWEEPS = 4
REACH = 2
PAD = 8
NEAR = 1408
FAR = 1088
GROUPS = 4
VMEM_LIMIT = 40 * 1024 * 1024
VMEM_WHOLE = 60 * 1024 * 1024


def shift_tile(value, by):
    tiles = lax.axis_size("tile")
    return lax.ppermute(value, "tile", [(t, (t + by) % tiles) for t in range(tiles)])


def swap_in_pair(value):
    wins = lax.axis_size("win")
    return lax.ppermute(value, "win", [(k, k ^ 1) for k in range(wins)])


def across_pairs(value):
    wins = lax.axis_size("win")
    pairs = [(k, k - 1 if k % 2 == 0 else k + 1) for k in range(1, wins - 1)]
    return lax.ppermute(value, "win", pairs)


def on_even(body_even, body_odd):
    odd = lax.rem(lax.axis_index("win"), 2)
    pl.when(odd == 0)(body_even)
    pl.when(odd == 1)(body_odd)


def params():
    return pltpu.CompilerParams(vmem_limit_bytes=VMEM_LIMIT)


def cost(flops, touched):
    return pl.CostEstimate(flops=flops, bytes_accessed=touched, transcendentals=0)


class Rows:
    def __init__(self, levels):
        base = SWEEPS * levels
        self.std = slice(base, base + SWEEPS)
        self.kappa = slice(base + SWEEPS, base + 2 * SWEEPS)
        self.weight = slice(base + 2 * SWEEPS, base + 2 * SWEEPS + REACH)
        self.code = slice(base + 2 * SWEEPS + REACH, base + 2 * SWEEPS + 2 * REACH)
        self.fields = base + 4 * SWEEPS
        self.count = self.fields + REACH * levels

    def mul(self, l):
        return slice(SWEEPS * l, SWEEPS * (l + 1))

    def inc(self, l):
        return slice(self.fields + REACH * l, self.fields + REACH * (l + 1))


def pack_one(levels, refs, out, from_end):
    inc, mul, std, kappa, weight, up, lev = refs
    wide = slice(PAD - SWEEPS, PAD) if from_end else slice(0, SWEEPS)
    thin = slice(PAD - REACH, PAD) if from_end else slice(0, REACH)
    spot = Rows(levels)
    for l in range(levels):
        out[spot.mul(l)] = mul[0, l, wide]
        out[spot.inc(l)] = inc[0, l, thin]
    out[spot.std] = std[wide]
    out[spot.kappa] = kappa[wide]
    out[spot.weight] = weight[thin]
    out[spot.code] = up[thin].astype(jnp.float32) * 3.0 + lev[thin].astype(jnp.float32)
    gap = slice(spot.code.stop, spot.fields)
    out[gap] = jnp.zeros_like(out[gap])


def pack_both(levels, *refs):
    pack_one(levels, refs[0:7], refs[14], True)
    pack_one(levels, refs[7:14], refs[15], False)


def pack(inc, mul, std, kappa, weight, up, lev):
    _, levels, width, rows = mul.shape
    arrays = [inc, mul, std, kappa, weight, up, lev]
    specs = []
    for block in (width // PAD - 1, 0):
        for a in arrays:
            lead = a.shape[:-2]
            index = (0,) * len(lead) + (block, 0)
            specs.append(
                pl.BlockSpec((*lead, PAD, rows), functools.partial(lambda index, i: index, index))
            )
    height = Rows(levels).count
    return pl.pallas_call(
        functools.partial(pack_both, levels),
        grid=(1,),
        in_specs=specs,
        out_specs=[pl.BlockSpec((height, rows), lambda i: (0, 0))] * 2,
        out_shape=[jax.ShapeDtypeStruct((height, rows), jnp.float32)] * 2,
        compiler_params=pltpu.CompilerParams(vmem_limit_bytes=VMEM_WHOLE),
        cost_estimate=cost(1000, 1000),
    )(*(arrays * 2))


def pick_kernel(even_source, odd_source, out):
    def copy(source):
        out[...] = source[: out.shape[0]]

    on_even(lambda: copy(even_source), lambda: copy(odd_source))


def pick(even_source, odd_source, count):
    vmem = pl.BlockSpec(memory_space=pltpu.VMEM)
    return pl.pallas_call(
        pick_kernel,
        in_specs=[vmem] * 2,
        out_specs=vmem,
        out_shape=jax.ShapeDtypeStruct((count, even_source.shape[1]), jnp.float32),
        compiler_params=params(),
        cost_estimate=cost(1000, 1000),
    )(even_source, odd_source)


def forward_kernel(near_early, far_early, inc, mul, before, after, near_out, far_out):
    _, levels, width, rows = mul.shape
    spot = Rows(levels)
    half = REACH * levels

    def copy(early, source, target):
        base = levels * width - early
        for l in range(levels):
            start = max(early - l * width, 0)
            if start < width:
                part = slice(l * width + start - early, (l + 1) * width - early)
                target[part] = source[0, l, start:]
            left = slice(base + REACH * l, base + REACH * (l + 1))
            right = slice(left.start + half, left.stop + half)
            if source is inc:
                target[left] = before[spot.inc(l)]
                target[right] = after[spot.inc(l)]
            else:
                first, last = before[spot.mul(l)], after[spot.mul(l)]
                target[left] = first[SWEEPS - REACH :]
                target[right] = last[:REACH]

    def even():
        copy(near_early, inc, near_out)
        copy(far_early, mul, far_out)

    def odd():
        copy(near_early, mul, near_out)
        copy(far_early, inc, far_out)

    on_even(even, odd)


def forward(near_early, far_early, inc, mul, before, after):
    _, levels, width, rows = mul.shape
    vmem = pl.BlockSpec(memory_space=pltpu.VMEM)
    heights = [levels * width - early + 2 * REACH * levels for early in (near_early, far_early)]
    return pl.pallas_call(
        functools.partial(forward_kernel, near_early, far_early),
        in_specs=[vmem] * 4,
        out_specs=[vmem] * 2,
        out_shape=[jax.ShapeDtypeStruct((h, rows), jnp.float32) for h in heights],
        compiler_params=params(),
        cost_estimate=cost(1000, 1000),
    )(inc, mul, before, after)


def covar_kernel(
    mul, inc, std, kappa, before, after, power, out, kappa_ext, field, smooth
):
    levels, width, rows = smooth.shape
    tall = width + 2 * PAD
    spot = Rows(levels)
    kappa_ext[...] = jnp.zeros_like(kappa_ext)
    field[...] = jnp.zeros_like(field)
    kappa_ext[PAD : PAD + width] = kappa[...]
    kappa_ext[PAD - SWEEPS : PAD] = before[spot.kappa]
    kappa_ext[PAD + width : PAD + width + SWEEPS] = after[spot.kappa]
    for l in range(levels):
        field[l, PAD - SWEEPS : PAD] = before[spot.std] * before[spot.mul(l)]
        field[l, PAD + width : PAD + width + SWEEPS] = after[spot.std] * after[spot.mul(l)]
    lane = lax.broadcasted_iota(jnp.int32, (tall, rows), 1)
    first, last = lane == 0, lane == rows - 1

    def one_level(l, carry):
        field[l, PAD : PAD + width] = std[...] * mul[0, l]
        value = field[l]
        for _ in range(SWEEPS):
            north = jnp.where(last, 0.0, pltpu.roll(value, rows - 1, 1))
            south = jnp.where(first, 0.0, pltpu.roll(value, 1, 1))
            around = pltpu.roll(value, 1, 0) + pltpu.roll(value, tall - 1, 0)
            value = value + kappa_ext[...] * ((around + (north + south)) - 4.0 * value)
        smooth[l] = value[PAD : PAD + width]
        return carry

    lax.fori_loop(0, levels, one_level, 0)
    step = 2 * PAD

    def one_block(b, carry):
        part = pl.ds(pl.multiple_of(b * step, step), step)
        fields = [smooth[m, part] for m in range(levels)]
        scale = std[part]
        for l in range(levels):
            total = power[l, 0] * fields[0]
            for m in range(1, levels):
                total = total + power[l, m] * fields[m]
            out[l, part] = scale * total + inc[0, l, part]
        return carry

    lax.fori_loop(0, width // step, one_block, 0)


def covar(mul, inc, std, kappa, before, after, power):
    _, levels, width, rows = mul.shape
    vmem = pl.BlockSpec(memory_space=pltpu.VMEM)
    return pl.pallas_call(
        covar_kernel,
        in_specs=[vmem] * 6 + [pl.BlockSpec(memory_space=pltpu.SMEM)],
        out_specs=vmem,
        out_shape=jax.ShapeDtypeStruct((levels, width, rows), jnp.float32),
        scratch_shapes=[
            pltpu.VMEM((width + 2 * PAD, rows), jnp.float32),
            pltpu.VMEM((levels, width + 2 * PAD, rows), jnp.float32),
            pltpu.VMEM((levels, width, rows), jnp.float32),
        ],
        compiler_params=params(),
        cost_estimate=cost(1000, 1000),
    )(mul, inc, std, kappa, before, after, power)


def fill_field(field, width, first, rest, known):
    levels = field.shape[0] - 2
    early = first.shape[0]
    zero = jnp.zeros_like(field[0])
    field[0] = zero
    field[levels + 1] = zero
    half = REACH * levels
    base = levels * width - early
    for l in range(levels):
        field[l + 1, :PAD] = zero[:PAD]
        field[l + 1, PAD + width :] = zero[:PAD]
        spans = [(0, width)]
        if l < known - 1:
            spans = [(0, 2 * PAD), (width - 2 * PAD, width)]
        for c0, c1 in spans:
            begin, end = l * width + c0, l * width + c1
            cut = min(max(early, begin), end)
            if cut > begin:
                field[l + 1, PAD + c0 : PAD + c0 + cut - begin] = first[begin:cut]
            if cut < end and rest is not None:
                field[l + 1, PAD + c1 - (end - cut) : PAD + c1] = rest[cut - early : end - early]
        if rest is not None:
            near = slice(base + REACH * l, base + REACH * (l + 1))
            field[l + 1, PAD - REACH : PAD] = rest[near]
            far = rest[near.start + half : near.stop + half]
            field[l + 1, PAD + width : PAD + width + REACH] = far


def primal_setup(levels, width, refs):
    level_field = refs["level_field"]
    zero = jnp.zeros_like(level_field[0])
    level_field[0] = zero
    level_field[levels + 1] = zero


def primal_levels(lo, hi, c0, c1, refs):
    base, weight, up, lev = (refs[name] for name in ("base", "weight", "up", "lev"))
    field, level_field, staged = (refs[name] for name in ("field", "level_field", "staged"))
    levels = base.shape[0]
    cols = slice(c0, c1)

    def shift(l, carry):
        step = up[cols]
        total = field[l + 1, PAD + c0 : PAD + c1]
        for j in (-2, -1, 1, 2):
            total = jnp.where(step == j, field[l + 1, PAD + c0 + j : PAD + c1 + j], total)
        level_field[l + 1, cols] = total
        return carry

    lax.fori_loop(max(lo - 1, 0), min(hi + 1, levels), shift, 0)

    def combine(l):
        pick = lev[cols]
        departed = jnp.where(
            pick == 0,
            level_field[l + 1, cols],
            jnp.where(pick == 1, level_field[l + 2, cols], level_field[l, cols]),
        )
        center = field[l + 1, PAD + c0 : PAD + c1]
        share = weight[cols]
        staged[l, cols] = base[l, cols] - ((1.0 - share) * center + share * departed)

    return combine


def dual_setup(levels, width, refs):
    spot = Rows(levels)
    left, right = slice(PAD - REACH, PAD), slice(PAD + width, PAD + width + REACH)
    for name in ("weight", "up", "lev"):
        extended = refs[name + "_ext"]
        extended[...] = jnp.zeros_like(extended)
        extended[PAD : PAD + width] = refs[name][...]
    for side, part in ((refs["before"], left), (refs["after"], right)):
        refs["weight_ext"][part] = side[spot.weight]
        code = side[spot.code]
        step = jnp.floor((code + 1.5) * (1.0 / 3.0))
        refs["up_ext"][part] = step.astype(jnp.int32)
        refs["lev_ext"][part] = (code - 3.0 * step).astype(jnp.int32)


def dual_levels(lo, hi, c0, c1, refs):
    mul, weight, field, staged = (refs[name] for name in ("mul", "weight", "field", "staged"))
    cols, around = slice(c0, c1), slice(c0, c1 + 2 * PAD)
    tall = c1 - c0 + 2 * PAD

    def one_level(l):
        pick = refs["lev_ext"][around]
        lifted = jnp.where(
            pick == 0,
            field[l + 1, around],
            jnp.where(pick == 1, field[l, around], field[l + 2, around]),
        )
        source = refs["weight_ext"][around] * lifted
        step = refs["up_ext"][around]
        total = jnp.where(step == 0, source, 0.0)
        for j in (-2, -1, 1, 2):
            total = total + pltpu.roll(jnp.where(step == j, source, 0.0), j % tall, 0)
        returned = total[PAD : PAD + c1 - c0]
        center = field[l + 1, PAD + c0 : PAD + c1]
        staged[l, cols] = mul[0, l, cols] - ((1.0 - weight[cols]) * center + returned)

    return one_level


def run_levels(lo, hi, body):
    lax.fori_loop(lo, hi, lambda l, carry: body(l) or carry, 0)


def produce(setup, make, known, refs, out, partial, sems):
    levels, width = refs["base"].shape[:2]
    fill_field(refs["field"], width, refs["first"], refs["rest"], known)
    staged, copies = refs["staged"], []

    def send(source, target):
        copy = pltpu.make_async_copy(source, target, sems.at[len(copies)])
        copy.start()
        copies.append(copy)

    if known:
        send(partial, out.at[0, pl.ds(0, known)])
    setup(levels, width, refs)
    body = make(known, levels, 0, width, refs)
    size = (levels - known) // 2
    for start in (known, known + size):
        stop = levels if start > known else start + size
        run_levels(start, stop, body)
        part = pl.ds(start, stop - start)
        send(staged.at[part], out.at[0, part])
    if known:
        spans = ((0, PAD), (width - PAD, width))
        for c0, c1 in spans:
            run_levels(0, known, make(0, known, c0, c1, refs))
        copies[0].wait()
        for c0, _ in spans:
            part, cols = pl.ds(0, known), pl.ds(c0, PAD)
            send(staged.at[part, cols], out.at[0, part, cols])
    for copy in copies[1 if known else 0 :]:
        copy.wait()


NAMES = ("base", "mul", "first", "rest", "before", "after", "weight", "up", "lev")
SCRATCH = ("field", "level_field", "weight_ext", "up_ext", "lev_ext", "staged")


def by_parity(primal_on_even, make_primal, make_dual):
    if primal_on_even:
        on_even(make_primal, make_dual)
    else:
        on_even(make_dual, make_primal)


def final_kernel(primal_on_even, known, *refs):
    named = dict(zip(NAMES, refs))
    refs = refs[len(NAMES) :]
    partial = None
    if known:
        partial, refs = refs[0], refs[3:]
    primal, dual, *scratch, sems = refs
    named.update(zip(SCRATCH, scratch))
    by_parity(
        primal_on_even,
        lambda: produce(primal_setup, primal_levels, known, named, primal, partial, sems),
        lambda: produce(dual_setup, dual_levels, known, named, dual, partial, sems),
    )


def scratch_shapes(levels, width, rows):
    tall = width + 2 * PAD
    return [
        pltpu.VMEM((levels + 2, tall, rows), jnp.float32),
        pltpu.VMEM((levels + 2, width, rows), jnp.float32),
        pltpu.VMEM((tall, rows), jnp.float32),
        pltpu.VMEM((tall, rows), jnp.int32),
        pltpu.VMEM((tall, rows), jnp.int32),
        pltpu.VMEM((levels, width, rows), jnp.float32),
        pltpu.SemaphoreType.DMA((5,)),
    ]


def final(primal_on_even, base, mul, pieces, before, after, columns, partial=None, done=()):
    _, levels, width, rows = mul.shape
    vmem = pl.BlockSpec(memory_space=pltpu.VMEM)
    anywhere = pl.BlockSpec(memory_space=pl.ANY)
    known = 0 if partial is None else partial.shape[0]
    extra = () if partial is None else (partial,)
    return pl.pallas_call(
        functools.partial(final_kernel, primal_on_even, known),
        in_specs=[vmem] * (9 + len(extra)) + [anywhere] * len(done),
        out_specs=[anywhere] * 2,
        out_shape=[jax.ShapeDtypeStruct(mul.shape, jnp.float32)] * 2,
        input_output_aliases={10: 0, 11: 1} if done else {},
        scratch_shapes=scratch_shapes(levels, width, rows),
        compiler_params=params(),
        cost_estimate=cost(1000, 1000),
    )(base, mul, *pieces, before, after, *columns, *extra, *done)


def partial_kernel(primal_on_even, *refs):
    names = [name for name in NAMES if name != "rest"]
    named = dict(zip(names, refs), rest=None)
    out, *scratch, _ = refs[len(names) :]
    named.update(zip(SCRATCH, scratch))
    named["staged"] = out
    levels, width = named["base"].shape[:2]

    def run(setup, make):
        fill_field(named["field"], width, named["first"], None, 0)
        setup(levels, width, named)
        run_levels(0, out.shape[0], make(0, out.shape[0], 0, width, named))

    by_parity(
        primal_on_even,
        lambda: run(primal_setup, primal_levels),
        lambda: run(dual_setup, dual_levels),
    )


def partial_final(primal_on_even, base, mul, first, before, after, columns):
    _, levels, width, rows = mul.shape
    vmem = pl.BlockSpec(memory_space=pltpu.VMEM)
    known = first.shape[0] // width - 1
    return pl.pallas_call(
        functools.partial(partial_kernel, primal_on_even),
        in_specs=[vmem] * 8,
        out_specs=vmem,
        out_shape=jax.ShapeDtypeStruct((known, width, rows), jnp.float32),
        scratch_shapes=scratch_shapes(levels, width, rows),
        compiler_params=params(),
        cost_estimate=cost(1000, 1000),
    )(base, mul, first, before, after, *columns)


def per_device(
    increments,
    multipliers,
    departure_weight,
    upstream,
    level_offset,
    diffusivity,
    std_dev,
    vertical_inverse,
):
    columns = (departure_weight, upstream, level_offset)
    _, levels, width, rows = multipliers.shape
    near_early, far_early = (n * levels * width // 2048 for n in (NEAR, FAR))
    inc_rows, mul_rows = increments.reshape(-1, rows), multipliers.reshape(-1, rows)
    even = lax.rem(lax.axis_index("win"), 2) == 0
    near_part = jnp.where(even, inc_rows[:near_early], mul_rows[:near_early])
    near_first = swap_in_pair(near_part)
    far_first = across_pairs(pick(mul_rows, inc_rows, far_early))
    to_right, to_left = pack(increments, multipliers, std_dev, diffusivity, *columns)
    before = shift_tile(to_right, 1)
    after = shift_tile(to_left, -1)
    near_out, far_out = forward(near_early, far_early, increments, multipliers, before, after)
    near_rest = swap_in_pair(near_out)
    far_rest = across_pairs(far_out)

    exact = dict(precision=lax.Precision.HIGHEST, preferred_element_type=jnp.float32)
    power = jnp.dot(vertical_inverse, vertical_inverse, **exact)
    power = jnp.dot(power, power, **exact)
    base = covar(multipliers, increments, std_dev, diffusivity, before, after, power)
    partial = partial_final(False, base, multipliers, near_first, before, after, columns)
    first_lev, partial = lax.optimization_barrier((level_offset, partial))
    columns_then = (departure_weight, upstream, first_lev)
    done = final(True, base, multipliers, (far_first, far_rest), before, after, columns_then)
    primal, dual = final(
        False, base, multipliers, (near_first, near_rest), before, after, columns, partial, done
    )
    return (primal, dual)


def solution(mesh):
    in_specs = (
        P("win", None, "tile", None),
        P("win", None, "tile", None),
        P("tile", None),
        P("tile", None),
        P("tile", None),
        P("tile", None),
        P("tile", None),
        P(),
    )
    out_specs = (P("win", None, "tile", None), P("win", None, "tile", None))
    return jax.shard_map(
        per_device, mesh=mesh, in_specs=in_specs, out_specs=out_specs, check_vma=False
    )
```

```python
import functools

import jax
import jax.numpy as jnp
from jax import lax
from jax.experimental import pallas as pl
from jax.experimental.pallas import tpu as pltpu
from jax.sharding import PartitionSpec as P

SWEEPS = 4
REACH = 2
PAD = 8
NEAR = 1536
FAR = 1088
GROUPS = 4
VMEM_LIMIT = 40 * 1024 * 1024
VMEM_WHOLE = 60 * 1024 * 1024


def shift_tile(value, by):
    tiles = lax.axis_size("tile")
    return lax.ppermute(value, "tile", [(t, (t + by) % tiles) for t in range(tiles)])


def swap_in_pair(value):
    wins = lax.axis_size("win")
    return lax.ppermute(value, "win", [(k, k ^ 1) for k in range(wins)])


def across_pairs(value):
    wins = lax.axis_size("win")
    pairs = [(k, k - 1 if k % 2 == 0 else k + 1) for k in range(1, wins - 1)]
    return lax.ppermute(value, "win", pairs)


def on_even(body_even, body_odd):
    odd = lax.rem(lax.axis_index("win"), 2)
    pl.when(odd == 0)(body_even)
    pl.when(odd == 1)(body_odd)


def params():
    return pltpu.CompilerParams(vmem_limit_bytes=VMEM_LIMIT)


def cost(flops, touched):
    return pl.CostEstimate(flops=flops, bytes_accessed=touched, transcendentals=0)


class Rows:
    def __init__(self, levels):
        base = SWEEPS * levels
        self.std = slice(base, base + SWEEPS)
        self.kappa = slice(base + SWEEPS, base + 2 * SWEEPS)
        self.weight = slice(base + 2 * SWEEPS, base + 2 * SWEEPS + REACH)
        self.code = slice(base + 2 * SWEEPS + REACH, base + 2 * SWEEPS + 2 * REACH)
        self.fields = base + 4 * SWEEPS
        self.count = self.fields + REACH * levels

    def mul(self, l):
        return slice(SWEEPS * l, SWEEPS * (l + 1))

    def inc(self, l):
        return slice(self.fields + REACH * l, self.fields + REACH * (l + 1))


def pack_one(levels, refs, out, from_end):
    inc, mul, std, kappa, weight, up, lev = refs
    wide = slice(PAD - SWEEPS, PAD) if from_end else slice(0, SWEEPS)
    thin = slice(PAD - REACH, PAD) if from_end else slice(0, REACH)
    spot = Rows(levels)
    for l in range(levels):
        out[spot.mul(l)] = mul[0, l, wide]
        out[spot.inc(l)] = inc[0, l, thin]
    out[spot.std] = std[wide]
    out[spot.kappa] = kappa[wide]
    out[spot.weight] = weight[thin]
    out[spot.code] = up[thin].astype(jnp.float32) * 3.0 + lev[thin].astype(jnp.float32)
    gap = slice(spot.code.stop, spot.fields)
    out[gap] = jnp.zeros_like(out[gap])


def pack_both(levels, *refs):
    pack_one(levels, refs[0:7], refs[14], True)
    pack_one(levels, refs[7:14], refs[15], False)


def pack(inc, mul, std, kappa, weight, up, lev):
    _, levels, width, rows = mul.shape
    arrays = [inc, mul, std, kappa, weight, up, lev]
    specs = []
    for block in (width // PAD - 1, 0):
        for a in arrays:
            lead = a.shape[:-2]
            index = (0,) * len(lead) + (block, 0)
            specs.append(
                pl.BlockSpec((*lead, PAD, rows), functools.partial(lambda index, i: index, index))
            )
    height = Rows(levels).count
    return pl.pallas_call(
        functools.partial(pack_both, levels),
        grid=(1,),
        in_specs=specs,
        out_specs=[pl.BlockSpec((height, rows), lambda i: (0, 0))] * 2,
        out_shape=[jax.ShapeDtypeStruct((height, rows), jnp.float32)] * 2,
        compiler_params=pltpu.CompilerParams(vmem_limit_bytes=VMEM_WHOLE),
        cost_estimate=cost(1000, 1000),
    )(*(arrays * 2))


def pick_kernel(even_source, odd_source, out):
    def copy(source):
        out[...] = source[: out.shape[0]]

    on_even(lambda: copy(even_source), lambda: copy(odd_source))


def pick(even_source, odd_source, count):
    vmem = pl.BlockSpec(memory_space=pltpu.VMEM)
    return pl.pallas_call(
        pick_kernel,
        in_specs=[vmem] * 2,
        out_specs=vmem,
        out_shape=jax.ShapeDtypeStruct((count, even_source.shape[1]), jnp.float32),
        compiler_params=params(),
        cost_estimate=cost(1000, 1000),
    )(even_source, odd_source)


def forward_kernel(near_early, far_early, inc, mul, before, after, near_out, far_out):
    _, levels, width, rows = mul.shape
    spot = Rows(levels)
    half = REACH * levels

    def copy(early, source, target):
        base = levels * width - early
        for l in range(levels):
            start = max(early - l * width, 0)
            if start < width:
                part = slice(l * width + start - early, (l + 1) * width - early)
                target[part] = source[0, l, start:]
            left = slice(base + REACH * l, base + REACH * (l + 1))
            right = slice(left.start + half, left.stop + half)
            if source is inc:
                target[left] = before[spot.inc(l)]
                target[right] = after[spot.inc(l)]
            else:
                first, last = before[spot.mul(l)], after[spot.mul(l)]
                target[left] = first[SWEEPS - REACH :]
                target[right] = last[:REACH]

    def even():
        copy(near_early, inc, near_out)
        copy(far_early, mul, far_out)

    def odd():
        copy(near_early, mul, near_out)
        copy(far_early, inc, far_out)

    on_even(even, odd)


def forward(near_early, far_early, inc, mul, before, after):
    _, levels, width, rows = mul.shape
    vmem = pl.BlockSpec(memory_space=pltpu.VMEM)
    heights = [levels * width - early + 2 * REACH * levels for early in (near_early, far_early)]
    return pl.pallas_call(
        functools.partial(forward_kernel, near_early, far_early),
        in_specs=[vmem] * 4,
        out_specs=[vmem] * 2,
        out_shape=[jax.ShapeDtypeStruct((h, rows), jnp.float32) for h in heights],
        compiler_params=params(),
        cost_estimate=cost(1000, 1000),
    )(inc, mul, before, after)


def covar_kernel(
    mul, inc, std, kappa, before, after, power, out, kappa_ext, field, smooth
):
    levels, width, rows = smooth.shape
    tall = width + 2 * PAD
    spot = Rows(levels)
    kappa_ext[...] = jnp.zeros_like(kappa_ext)
    field[...] = jnp.zeros_like(field)
    kappa_ext[PAD : PAD + width] = kappa[...]
    kappa_ext[PAD - SWEEPS : PAD] = before[spot.kappa]
    kappa_ext[PAD + width : PAD + width + SWEEPS] = after[spot.kappa]
    for l in range(levels):
        field[l, PAD - SWEEPS : PAD] = before[spot.std] * before[spot.mul(l)]
        field[l, PAD + width : PAD + width + SWEEPS] = after[spot.std] * after[spot.mul(l)]
    lane = lax.broadcasted_iota(jnp.int32, (tall, rows), 1)
    first, last = lane == 0, lane == rows - 1

    def one_level(l, carry):
        field[l, PAD : PAD + width] = std[...] * mul[0, l]
        value = field[l]
        for _ in range(SWEEPS):
            north = jnp.where(last, 0.0, pltpu.roll(value, rows - 1, 1))
            south = jnp.where(first, 0.0, pltpu.roll(value, 1, 1))
            around = pltpu.roll(value, 1, 0) + pltpu.roll(value, tall - 1, 0)
            value = value + kappa_ext[...] * ((around + (north + south)) - 4.0 * value)
        smooth[l] = value[PAD : PAD + width]
        return carry

    lax.fori_loop(0, levels, one_level, 0)
    step = 2 * PAD

    def one_block(b, carry):
        part = pl.ds(pl.multiple_of(b * step, step), step)
        fields = [smooth[m, part] for m in range(levels)]
        scale = std[part]
        for l in range(levels):
            total = power[l, 0] * fields[0]
            for m in range(1, levels):
                total = total + power[l, m] * fields[m]
            out[l, part] = scale * total + inc[0, l, part]
        return carry

    lax.fori_loop(0, width // step, one_block, 0)


def covar(mul, inc, std, kappa, before, after, power):
    _, levels, width, rows = mul.shape
    vmem = pl.BlockSpec(memory_space=pltpu.VMEM)
    return pl.pallas_call(
        covar_kernel,
        in_specs=[vmem] * 6 + [pl.BlockSpec(memory_space=pltpu.SMEM)],
        out_specs=vmem,
        out_shape=jax.ShapeDtypeStruct((levels, width, rows), jnp.float32),
        scratch_shapes=[
            pltpu.VMEM((width + 2 * PAD, rows), jnp.float32),
            pltpu.VMEM((levels, width + 2 * PAD, rows), jnp.float32),
            pltpu.VMEM((levels, width, rows), jnp.float32),
        ],
        compiler_params=params(),
        cost_estimate=cost(1000, 1000),
    )(mul, inc, std, kappa, before, after, power)


def fill_field(field, width, first, rest, known):
    levels = field.shape[0] - 2
    early = first.shape[0]
    zero = jnp.zeros_like(field[0])
    field[0] = zero
    field[levels + 1] = zero
    half = REACH * levels
    base = levels * width - early
    for l in range(levels):
        field[l + 1, :PAD] = zero[:PAD]
        field[l + 1, PAD + width :] = zero[:PAD]
        spans = [(0, width)]
        if l < known - 1:
            spans = [(0, 2 * PAD), (width - 2 * PAD, width)]
        for c0, c1 in spans:
            begin, end = l * width + c0, l * width + c1
            cut = min(max(early, begin), end)
            if cut > begin:
                field[l + 1, PAD + c0 : PAD + c0 + cut - begin] = first[begin:cut]
            if cut < end and rest is not None:
                field[l + 1, PAD + c1 - (end - cut) : PAD + c1] = rest[cut - early : end - early]
        if rest is not None:
            near = slice(base + REACH * l, base + REACH * (l + 1))
            field[l + 1, PAD - REACH : PAD] = rest[near]
            far = rest[near.start + half : near.stop + half]
            field[l + 1, PAD + width : PAD + width + REACH] = far


def primal_setup(levels, width, refs):
    level_field = refs["level_field"]
    zero = jnp.zeros_like(level_field[0])
    level_field[0] = zero
    level_field[levels + 1] = zero


def primal_levels(lo, hi, c0, c1, refs):
    base, weight, up, lev = (refs[name] for name in ("base", "weight", "up", "lev"))
    field, level_field, staged = (refs[name] for name in ("field", "level_field", "staged"))
    levels = base.shape[0]
    cols = slice(c0, c1)

    def shift(l, carry):
        step = up[cols]
        total = field[l + 1, PAD + c0 : PAD + c1]
        for j in (-2, -1, 1, 2):
            total = jnp.where(step == j, field[l + 1, PAD + c0 + j : PAD + c1 + j], total)
        level_field[l + 1, cols] = total
        return carry

    lax.fori_loop(max(lo - 1, 0), min(hi + 1, levels), shift, 0)

    def combine(l):
        pick = lev[cols]
        departed = jnp.where(
            pick == 0,
            level_field[l + 1, cols],
            jnp.where(pick == 1, level_field[l + 2, cols], level_field[l, cols]),
        )
        center = field[l + 1, PAD + c0 : PAD + c1]
        share = weight[cols]
        staged[l, cols] = base[l, cols] - ((1.0 - share) * center + share * departed)

    return combine


def dual_setup(levels, width, refs):
    spot = Rows(levels)
    left, right = slice(PAD - REACH, PAD), slice(PAD + width, PAD + width + REACH)
    for name in ("weight", "up", "lev"):
        extended = refs[name + "_ext"]
        extended[...] = jnp.zeros_like(extended)
        extended[PAD : PAD + width] = refs[name][...]
    for side, part in ((refs["before"], left), (refs["after"], right)):
        refs["weight_ext"][part] = side[spot.weight]
        code = side[spot.code]
        step = jnp.floor((code + 1.5) * (1.0 / 3.0))
        refs["up_ext"][part] = step.astype(jnp.int32)
        refs["lev_ext"][part] = (code - 3.0 * step).astype(jnp.int32)


def dual_levels(lo, hi, c0, c1, refs):
    mul, weight, field, staged = (refs[name] for name in ("mul", "weight", "field", "staged"))
    cols, around = slice(c0, c1), slice(c0, c1 + 2 * PAD)
    tall = c1 - c0 + 2 * PAD

    def one_level(l):
        pick = refs["lev_ext"][around]
        lifted = jnp.where(
            pick == 0,
            field[l + 1, around],
            jnp.where(pick == 1, field[l, around], field[l + 2, around]),
        )
        source = refs["weight_ext"][around] * lifted
        step = refs["up_ext"][around]
        total = jnp.where(step == 0, source, 0.0)
        for j in (-2, -1, 1, 2):
            total = total + pltpu.roll(jnp.where(step == j, source, 0.0), j % tall, 0)
        returned = total[PAD : PAD + c1 - c0]
        center = field[l + 1, PAD + c0 : PAD + c1]
        staged[l, cols] = mul[0, l, cols] - ((1.0 - weight[cols]) * center + returned)

    return one_level


def run_levels(lo, hi, body):
    lax.fori_loop(lo, hi, lambda l, carry: body(l) or carry, 0)


def produce(setup, make, known, refs, out, partial, sems):
    levels, width = refs["base"].shape[:2]
    fill_field(refs["field"], width, refs["first"], refs["rest"], known)
    staged, copies = refs["staged"], []

    def send(source, target):
        copy = pltpu.make_async_copy(source, target, sems.at[len(copies)])
        copy.start()
        copies.append(copy)

    if known:
        send(partial, out.at[0, pl.ds(0, known)])
    setup(levels, width, refs)
    body = make(known, levels, 0, width, refs)
    size = (levels - known) // 2
    for start in (known, known + size):
        stop = levels if start > known else start + size
        run_levels(start, stop, body)
        part = pl.ds(start, stop - start)
        send(staged.at[part], out.at[0, part])
    if known:
        spans = ((0, PAD), (width - PAD, width))
        for c0, c1 in spans:
            run_levels(0, known, make(0, known, c0, c1, refs))
        copies[0].wait()
        for c0, _ in spans:
            part, cols = pl.ds(0, known), pl.ds(c0, PAD)
            send(staged.at[part, cols], out.at[0, part, cols])
    for copy in copies[1 if known else 0 :]:
        copy.wait()


NAMES = ("base", "mul", "first", "rest", "before", "after", "weight", "up", "lev")
SCRATCH = ("field", "level_field", "weight_ext", "up_ext", "lev_ext", "staged")


def by_parity(primal_on_even, make_primal, make_dual):
    if primal_on_even:
        on_even(make_primal, make_dual)
    else:
        on_even(make_dual, make_primal)


def final_kernel(primal_on_even, known, *refs):
    named = dict(zip(NAMES, refs))
    refs = refs[len(NAMES) :]
    partial = None
    if known:
        partial, refs = refs[0], refs[3:]
    primal, dual, *scratch, sems = refs
    named.update(zip(SCRATCH, scratch))
    by_parity(
        primal_on_even,
        lambda: produce(primal_setup, primal_levels, known, named, primal, partial, sems),
        lambda: produce(dual_setup, dual_levels, known, named, dual, partial, sems),
    )


def scratch_shapes(levels, width, rows):
    tall = width + 2 * PAD
    return [
        pltpu.VMEM((levels + 2, tall, rows), jnp.float32),
        pltpu.VMEM((levels + 2, width, rows), jnp.float32),
        pltpu.VMEM((tall, rows), jnp.float32),
        pltpu.VMEM((tall, rows), jnp.int32),
        pltpu.VMEM((tall, rows), jnp.int32),
        pltpu.VMEM((levels, width, rows), jnp.float32),
        pltpu.SemaphoreType.DMA((5,)),
    ]


def final(primal_on_even, base, mul, pieces, before, after, columns, partial=None, done=()):
    _, levels, width, rows = mul.shape
    vmem = pl.BlockSpec(memory_space=pltpu.VMEM)
    anywhere = pl.BlockSpec(memory_space=pl.ANY)
    known = 0 if partial is None else partial.shape[0]
    extra = () if partial is None else (partial,)
    return pl.pallas_call(
        functools.partial(final_kernel, primal_on_even, known),
        in_specs=[vmem] * (9 + len(extra)) + [anywhere] * len(done),
        out_specs=[anywhere] * 2,
        out_shape=[jax.ShapeDtypeStruct(mul.shape, jnp.float32)] * 2,
        input_output_aliases={10: 0, 11: 1} if done else {},
        scratch_shapes=scratch_shapes(levels, width, rows),
        compiler_params=params(),
        cost_estimate=cost(1000, 1000),
    )(base, mul, *pieces, before, after, *columns, *extra, *done)


def partial_kernel(primal_on_even, *refs):
    names = [name for name in NAMES if name != "rest"]
    named = dict(zip(names, refs), rest=None)
    out, *scratch, _ = refs[len(names) :]
    named.update(zip(SCRATCH, scratch))
    named["staged"] = out
    levels, width = named["base"].shape[:2]

    def run(setup, make):
        fill_field(named["field"], width, named["first"], None, 0)
        setup(levels, width, named)
        run_levels(0, out.shape[0], make(0, out.shape[0], 0, width, named))

    by_parity(
        primal_on_even,
        lambda: run(primal_setup, primal_levels),
        lambda: run(dual_setup, dual_levels),
    )


def partial_final(primal_on_even, base, mul, first, before, after, columns):
    _, levels, width, rows = mul.shape
    vmem = pl.BlockSpec(memory_space=pltpu.VMEM)
    known = first.shape[0] // width - 1
    return pl.pallas_call(
        functools.partial(partial_kernel, primal_on_even),
        in_specs=[vmem] * 8,
        out_specs=vmem,
        out_shape=jax.ShapeDtypeStruct((known, width, rows), jnp.float32),
        scratch_shapes=scratch_shapes(levels, width, rows),
        compiler_params=params(),
        cost_estimate=cost(1000, 1000),
    )(base, mul, first, before, after, *columns)


def per_device(
    increments,
    multipliers,
    departure_weight,
    upstream,
    level_offset,
    diffusivity,
    std_dev,
    vertical_inverse,
):
    columns = (departure_weight, upstream, level_offset)
    _, levels, width, rows = multipliers.shape
    near_early, far_early = (n * levels * width // 2048 for n in (NEAR, FAR))
    inc_rows, mul_rows = increments.reshape(-1, rows), multipliers.reshape(-1, rows)
    even = lax.rem(lax.axis_index("win"), 2) == 0
    near_part = jnp.where(even, inc_rows[:near_early], mul_rows[:near_early])
    near_first = swap_in_pair(near_part)
    far_first = across_pairs(pick(mul_rows, inc_rows, far_early))
    to_right, to_left = pack(increments, multipliers, std_dev, diffusivity, *columns)
    before = shift_tile(to_right, 1)
    after = shift_tile(to_left, -1)
    near_out, far_out = forward(near_early, far_early, increments, multipliers, before, after)
    near_rest = swap_in_pair(near_out)
    far_rest = across_pairs(far_out)

    exact = dict(precision=lax.Precision.HIGHEST, preferred_element_type=jnp.float32)
    power = jnp.dot(vertical_inverse, vertical_inverse, **exact)
    power = jnp.dot(power, power, **exact)
    base = covar(multipliers, increments, std_dev, diffusivity, before, after, power)
    partial = partial_final(False, base, multipliers, near_first, before, after, columns)
    first_lev, partial = lax.optimization_barrier((level_offset, partial))
    columns_then = (departure_weight, upstream, first_lev)
    done = final(True, base, multipliers, (far_first, far_rest), before, after, columns_then)
    primal, dual = final(
        False, base, multipliers, (near_first, near_rest), before, after, columns, partial, done
    )
    return (primal, dual)


def solution(mesh):
    in_specs = (
        P("win", None, "tile", None),
        P("win", None, "tile", None),
        P("tile", None),
        P("tile", None),
        P("tile", None),
        P("tile", None),
        P("tile", None),
        P(),
    )
    out_specs = (P("win", None, "tile", None), P("win", None, "tile", None))
    return jax.shard_map(
        per_device, mesh=mesh, in_specs=in_specs, out_specs=out_specs, check_vma=False
    )
```
